32 devices in a mesh: dp: 2 (over y), expert: 4 (over z), hidden: 4 (over x, core).
Axes of the slice: x: 2, y: 2, z: 4, core: 2. Of those that a mesh axis runs over, the one named last changes fastest.
Arguments:
- frames: bfloat16 [4, 2048, 512], P('dp', 'hidden', 'expert'), may hold values from -8 to 8
- cotangent: bfloat16 [4, 2048, 512], P('dp', 'hidden', 'expert'), may hold values from -6 to 6
- lengths: int32 [4, 4], P('dp'), may hold values from 1 to 1569, 2048 in all within a row
- routes: int32 [4, 2048, 1], P('dp', 'hidden'), may hold values from 0 to 7; in each aligned block of 512 rows (0 to 511, 512 to 1023, ..., all dimensions but the last counted through in order) at most 96 rows name the same one
- entry_weights: float32 [2, 512, 9, 512], P(None, ('dp', 'hidden'), None, 'expert'), may hold values from -0.25 to 0.25
- entry_moment: float32 [2, 512, 9, 512], P(None, ('dp', 'hidden'), None, 'expert'), may hold values from -8 to 8
- entry_square: float32 [2, 512, 9, 512], P(None, ('dp', 'hidden'), None, 'expert'), may hold values from 3.6864 to 14.7456
- exit_weights: float32 [2, 6, 512, 512], P(None, None, 'expert', ('dp', 'hidden')), may hold values from -0.25 to 0.25
- exit_moment: float32 [2, 6, 512, 512], P(None, None, 'expert', ('dp', 'hidden')), may hold values from -12 to 12
- exit_square: float32 [2, 6, 512, 512], P(None, None, 'expert', ('dp', 'hidden')), may hold values from 6.5536 to 26.2144
- upward_weights: float32 [2, 8, 512, 2048], P(None, 'expert', 'dp', 'hidden'), may hold values from -0.25 to 0.25
- upward_moment: float32 [2, 8, 512, 2048], P(None, 'expert', 'dp', 'hidden'), may hold values from -2.5 to 2.5
- upward_square: float32 [2, 8, 512, 2048], P(None, 'expert', 'dp', 'hidden'), may hold values from 0.262144 to 1.048576
- downward_weights: float32 [2, 8, 2048, 512], P(None, 'expert', 'hidden', 'dp'), may hold values from -1 to 1
- downward_moment: float32 [2, 8, 2048, 512], P(None, 'expert', 'hidden', 'dp'), may hold values from -0.75 to 0.75
- downward_square: float32 [2, 8, 2048, 512], P(None, 'expert', 'hidden', 'dp'), may hold values from 0.0262144 to 0.1048576
- norm_gains: float32 [2, 5, 512], P(None, None, 'expert'), may hold values from 0.5 to 1.5
- gains_moment: float32 [2, 5, 512], P(None, None, 'expert'), may hold values from -32 to 32
- gains_square: float32 [2, 5, 512], P(None, None, 'expert'), may hold values from 40.96 to 163.84
- conv_kernel: float32 [2, 15, 512], P(None, None, 'expert'), may hold values from -1.5 to 1.5
- kernel_moment: float32 [2, 15, 512], P(None, None, 'expert'), may hold values from -12 to 12
- kernel_square: float32 [2, 15, 512], P(None, None, 'expert'), may hold values from 6.5536 to 26.2144
- router_weights: float32 [2, 512, 8], P(None, 'expert'), may hold values from -0.25 to 0.25
- router_moment: float32 [2, 512, 8], P(None, 'expert'), may hold values from -320 to 320
- router_square: float32 [2, 512, 8], P(None, 'expert'), may hold values from 491.52 to 1966.08
Outputs:
- encoded: float32 [4, 2048, 512], P('dp', 'hidden', 'expert')
- input_gradient: float32 [4, 2048, 512], P('dp', 'hidden', 'expert')
- entry_updated: float32 [2, 512, 9, 512], P(None, ('dp', 'hidden'), None, 'expert')
- entry_momentum: float32 [2, 512, 9, 512], P(None, ('dp', 'hidden'), None, 'expert')
- entry_squares: float32 [2, 512, 9, 512], P(None, ('dp', 'hidden'), None, 'expert')
- exit_updated: float32 [2, 6, 512, 512], P(None, None, 'expert', ('dp', 'hidden'))
- exit_momentum: float32 [2, 6, 512, 512], P(None, None, 'expert', ('dp', 'hidden'))
- exit_squares: float32 [2, 6, 512, 512], P(None, None, 'expert', ('dp', 'hidden'))
- upward_updated: float32 [2, 8, 512, 2048], P(None, 'expert', 'dp', 'hidden')
- upward_momentum: float32 [2, 8, 512, 2048], P(None, 'expert', 'dp', 'hidden')
- upward_squares: float32 [2, 8, 512, 2048], P(None, 'expert', 'dp', 'hidden')
- downward_updated: float32 [2, 8, 2048, 512], P(None, 'expert', 'hidden', 'dp')
- downward_momentum: float32 [2, 8, 2048, 512], P(None, 'expert', 'hidden', 'dp')
- downward_squares: float32 [2, 8, 2048, 512], P(None, 'expert', 'hidden', 'dp')
- gains_updated: float32 [2, 5, 512], P(None, None, 'expert')
- gains_momentum: float32 [2, 5, 512], P(None, None, 'expert')
- gains_squares: float32 [2, 5, 512], P(None, None, 'expert')
- kernel_updated: float32 [2, 15, 512], P(None, None, 'expert')
- kernel_momentum: float32 [2, 15, 512], P(None, None, 'expert')
- kernel_squares: float32 [2, 15, 512], P(None, None, 'expert')
- router_updated: float32 [2, 512, 8], P(None, 'expert')
- router_momentum: float32 [2, 512, 8], P(None, 'expert')
- router_squares: float32 [2, 512, 8], P(None, 'expert')
The draws below stay inside these ranges and needn't reach their ends.
Inputs may be any that keep to these rules, and one draw needn't show every extreme that they name: Each row of 4 lengths sums to 2048, and its largest is exactly 1569. `routes`: within each aligned block of 512 rows (the frames of one bin on one index of hidden), no expert is named more than 96 times, and some block names one expert exactly 96 times.
All inputs are finite; a program needn't handle non-finite values.
Results may differ from the reference program's by a relative error of at most 0.025.
Values may be sent and summed in bfloat16 or wider, within the bound.
No kernel may reach another device: no remote copies, remote signals or barrier semaphores. Data moves between devices by JAX's collectives and lax.ppermute only.
A program may use at most 256 MiB of HBM per device.

```python
import math
import jax
import jax.numpy as jnp
import numpy as np
from jax import lax

D = 512
HEADS = 8
HD = 64
EFF = 2048
EXPERTS = 8
KER = 15
LAYERS = 2
UTTS = 4
BIN = 2048
STEP = 5
BINS = 4
QF = 512
CAP = 96
LONGEST = 1569
FRAMES = 8192
N_HIDDEN = 4


def draw_frames(key, part):
    key = jax.random.fold_in(key, 11)
    ramp = jnp.arange(D, dtype=jnp.float32) / D
    base = jnp.clip(jax.random.normal(key, (BINS, BIN, D), jnp.float32), -4.0, 4.0)
    scale = 0.6 + 1.2 * ramp
    return (base * scale).astype(jnp.bfloat16)


def block_levels(rng, extent, cuts, smallest, largest):
    def one(dim, blocks):
        steps = jax.random.uniform(jax.random.fold_in(jax.random.fold_in(rng, 6), dim), (blocks,), jnp.float32, smallest / len(cuts), largest / len(cuts))
        return jnp.repeat(jnp.exp(steps), extent[dim] // blocks).reshape((-1,) + (1,) * (len(extent) - dim - 1))

    factor_of = one(*cuts[0])
    for cut in cuts[1:]:
        factor_of = factor_of * one(*cut)
    return factor_of


def profile(count, total, limit, lean):
    portions = [(1 << 20) // math.isqrt(grade ** lean) + 1 for grade in range(2, count + 1)]
    surplus, holding = total - limit - (count - 1), [1] * (count - 1)
    while surplus > 0:
        movable = [i for i in range(count - 1) if holding[i] < limit]
        mass, budget = sum([portions[i] for i in movable]), surplus
        for i in movable:
            more = min(limit - holding[i], max(1, budget * portions[i] // mass), surplus)
            holding[i] = holding[i] + more
            surplus = surplus - more
    return np.array([limit] + holding)


def ragged(key, count, total, most, lean):
    if count == 2:
        one = jax.random.randint(key, (), max(1, total - most), min(most, total - 1) + 1)
        return jnp.stack([one, total - one])
    sizes = jnp.asarray(profile(count, total, most, lean), jnp.int32)
    couples = (count - 1) // 2
    donor, sink = sizes[1:1 + 2 * couples:2], sizes[2:2 + 2 * couples:2]
    slack = jnp.minimum(donor - 1, most - sink)
    shifted = jax.random.randint(jax.random.fold_in(key, 1), (couples,), 0, 1 << 20) % (slack + 1)
    sizes = sizes.at[1:1 + 2 * couples:2].set(donor - shifted).at[2:2 + 2 * couples:2].set(sink + shifted)
    return sizes[jax.random.permutation(jax.random.fold_in(key, 2), count)]


def deal_out(rng, own, number, rows, number_of, top, most, slope):
    ranking = jax.random.permutation(rng, number_of)
    crowded, usual = portions_of(number_of, rows * top, most, slope, True), portions_of(number_of, rows * top, most, slope, False)
    places = jnp.arange(number_of)

    def named(tallies, turn):
        used = int((tallies > 0).sum())
        fixed = max(1, used // 4)
        shifted = fixed + (places - fixed + turn * (used - fixed)) % max(1, number_of - fixed)
        return jnp.zeros((number_of,), jnp.int32).at[ranking[jnp.where(places < fixed, places, shifted)]].set(jnp.asarray(tallies, jnp.int32))

    tallies = jnp.where(number % 4 == 0, named(crowded, number // 4), named(usual, number - number // 4 - 1))
    mixed = jax.random.permutation(jax.random.fold_in(own, 3), number_of)
    giver, sink = mixed[0:number_of // 2 * 2:2], mixed[1:number_of // 2 * 2:2]
    room = jnp.minimum(tallies[giver] - 1, most - tallies[sink]) // 2
    room = jnp.where((giver == ranking[0]) | (sink == ranking[0]) | (tallies[sink] == 0), 0, jnp.maximum(room, 0))
    shifted = jax.random.randint(jax.random.fold_in(own, 4), (number_of // 2,), 0, 1 << 20) % (room + 1)
    tallies = tallies.at[giver].add(-shifted).at[sink].add(shifted)
    labels = jnp.searchsorted(jnp.cumsum(tallies), jnp.arange(rows * top), side="right").astype(jnp.int32)
    listing = labels.reshape(top, rows).T
    listing = listing[jax.random.permutation(jax.random.fold_in(own, 1), rows)]
    turn = jax.random.randint(jax.random.fold_in(own, 2), (rows, 1), 0, top)
    return jnp.take_along_axis(listing, (jnp.arange(top)[None, :] + turn) % top, axis=1)


def portions_of(number_of, total, bound, lean, full):
    weights = [(1 << 20) // math.isqrt(rank ** lean) + 1 for rank in range(1, number_of + 1)]
    largest = bound if full else min(bound, max(-(-total // number_of), total * weights[0] // sum(weights)))
    least = 1 if total - largest >= number_of - 1 else 0
    holding, rest = [largest] + [least] * (number_of - 1), total - largest - least * (number_of - 1)
    while rest > 0:
        free = [i for i in range(1, number_of) if holding[i] < largest] or [i for i in range(1, number_of) if holding[i] < bound]
        pool, budget = sum([weights[i] for i in free]), rest
        for i in free:
            more = min(bound - holding[i], max(1, budget * weights[i] // pool), rest)
            holding[i] = holding[i] + more
            rest = rest - more
    return np.array(holding)


def noise(rng, extent, spread, reach, shards=(), held_as=jnp.bfloat16):
    factor_of = block_levels(rng, extent, shards, -0.22, 0.18) if shards else 1.0
    entries = jax.random.normal(rng, extent, jnp.float32) * spread * factor_of
    return jnp.minimum(jnp.maximum(entries, -reach), reach).astype(held_as)


def setup_inputs(seed: int = 0) -> dict:
    seeds = jax.random.split(jax.random.key(seed), 26)
    frames = draw_frames(jax.random.fold_in(seeds[25], 71), 0)
    cotangent = noise(seeds[1], (BINS, BIN, D), 1.0, 6.0, ((0, 2), (1, 4), (2, 4)))
    lengths = jax.vmap(lambda own: ragged(own, UTTS, BIN, LONGEST, 1))(jax.random.split(seeds[2], BINS)).reshape((BINS, UTTS)).astype(jnp.int32)
    routes_keys = jax.random.split(jax.random.fold_in(seeds[3], 1), BINS * BIN // QF)
    routes_turns = jax.random.permutation(jax.random.fold_in(seeds[3], 3), BINS * BIN // QF)
    routes = jax.vmap(lambda own, number: deal_out(jax.random.fold_in(seeds[3], 2), own, number, QF, EXPERTS, 1, CAP, 1))(routes_keys, routes_turns).reshape((BINS, BIN, 1))
    entry_weights = noise(seeds[4], (LAYERS, D, 9, D), D ** -0.5, 0.25, ((1, 8), (3, 4)), jnp.float32)
    entry_moment = noise(seeds[5], (LAYERS, D, 9, D), (0.0167 * FRAMES ** 0.5), 8.0, ((1, 8), (3, 4)), jnp.float32)
    entry_square = jnp.clip(jnp.exp(math.log(14.7456) - 1.3862944 * jax.random.uniform(seeds[6], (LAYERS, D, 9, D), jnp.float32) ** block_levels(seeds[6], (LAYERS, D, 9, D), ((1, 8), (3, 4)), -0.2, 0.2)), 3.6864, 14.7456)
    exit_weights = noise(seeds[7], (LAYERS, 6, D, D), D ** -0.5, 0.25, ((2, 4), (3, 8)), jnp.float32)
    exit_moment = noise(seeds[8], (LAYERS, 6, D, D), (0.022 * FRAMES ** 0.5), 12.0, ((2, 4), (3, 8)), jnp.float32)
    exit_square = jnp.clip(jnp.exp(math.log(26.2144) - 1.3862944 * jax.random.uniform(seeds[9], (LAYERS, 6, D, D), jnp.float32) ** block_levels(seeds[9], (LAYERS, 6, D, D), ((2, 4), (3, 8)), -0.2, 0.2)), 6.5536, 26.2144)
    upward_weights = noise(seeds[10], (LAYERS, EXPERTS, D, EFF), D ** -0.5, 0.25, ((1, 4), (2, 2), (3, 4)), jnp.float32)
    upward_moment = noise(seeds[11], (LAYERS, EXPERTS, D, EFF), (0.0044 * FRAMES ** 0.5), 2.5, ((1, 4), (2, 2), (3, 4)), jnp.float32)
    upward_square = jnp.clip(jnp.exp(math.log(1.048576) - 1.3862944 * jax.random.uniform(seeds[12], (LAYERS, EXPERTS, D, EFF), jnp.float32) ** block_levels(seeds[12], (LAYERS, EXPERTS, D, EFF), ((1, 4), (2, 2), (3, 4)), -0.2, 0.2)), 0.262144, 1.048576)
    downward_weights = noise(seeds[13], (LAYERS, EXPERTS, EFF, D), (max(EFF // 64, 1)) ** -0.5, 1.0, ((1, 4), (2, 4), (3, 2)), jnp.float32)
    downward_moment = noise(seeds[14], (LAYERS, EXPERTS, EFF, D), (0.0014 * FRAMES ** 0.5), 0.75, ((1, 4), (2, 4), (3, 2)), jnp.float32)
    downward_square = jnp.clip(jnp.exp(math.log(0.1048576) - 1.3862944 * jax.random.uniform(seeds[15], (LAYERS, EXPERTS, EFF, D), jnp.float32) ** block_levels(seeds[15], (LAYERS, EXPERTS, EFF, D), ((1, 4), (2, 4), (3, 2)), -0.2, 0.2)), 0.0262144, 0.1048576)
    norm_gains = jnp.clip(1.0 + 0.1 * jax.random.normal(seeds[16], (LAYERS, 5, D), jnp.float32), 0.5, 1.5)
    gains_moment = noise(seeds[17], (LAYERS, 5, D), (0.055 * FRAMES ** 0.5), 32.0, ((2, 4),), jnp.float32)
    gains_square = jnp.clip(jnp.exp(math.log(163.84) - 1.3862944 * jax.random.uniform(seeds[18], (LAYERS, 5, D), jnp.float32) ** block_levels(seeds[18], (LAYERS, 5, D), ((2, 4),), -0.2, 0.2)), 40.96, 163.84)
    conv_kernel = noise(seeds[19], (LAYERS, KER, D), KER ** -0.5, 1.5, ((2, 4),), jnp.float32)
    kernel_moment = noise(seeds[20], (LAYERS, KER, D), (0.022 * FRAMES ** 0.5), 12.0, ((2, 4),), jnp.float32)
    kernel_square = jnp.clip(jnp.exp(math.log(26.2144) - 1.3862944 * jax.random.uniform(seeds[21], (LAYERS, KER, D), jnp.float32) ** block_levels(seeds[21], (LAYERS, KER, D), ((2, 4),), -0.2, 0.2)), 6.5536, 26.2144)
    router_weights = noise(seeds[22], (LAYERS, D, EXPERTS), D ** -0.5, 0.25, ((1, 4),), jnp.float32)
    router_moment = noise(seeds[23], (LAYERS, D, EXPERTS), (0.55 * FRAMES ** 0.5), 320.0, ((1, 4),), jnp.float32)
    router_square = jnp.clip(jnp.exp(math.log(1966.08) - 1.3862944 * jax.random.uniform(seeds[24], (LAYERS, D, EXPERTS), jnp.float32) ** block_levels(seeds[24], (LAYERS, D, EXPERTS), ((1, 4),), -0.2, 0.2)), 491.52, 1966.08)
    return {"frames": frames, "cotangent": cotangent, "lengths": lengths, "routes": routes, "entry_weights": entry_weights, "entry_moment": entry_moment, "entry_square": entry_square, "exit_weights": exit_weights, "exit_moment": exit_moment, "exit_square": exit_square, "upward_weights": upward_weights, "upward_moment": upward_moment, "upward_square": upward_square, "downward_weights": downward_weights, "downward_moment": downward_moment, "downward_square": downward_square, "norm_gains": norm_gains, "gains_moment": gains_moment, "gains_square": gains_square, "conv_kernel": conv_kernel, "kernel_moment": kernel_moment, "kernel_square": kernel_square, "router_weights": router_weights, "router_moment": router_moment, "router_square": router_square}


EPS = 1e-05
NEG = -1e+30
BETA_ONE = 0.9
BETA_TWO = 0.98
ADAM_EPS = 1e-08
DECAY = 0.01
BEST = lax.Precision.HIGHEST

@jax.custom_vjp
def low(v):
    return lax.optimization_barrier(v.astype(jnp.bfloat16)).astype(jnp.float32)

@jax.custom_vjp
def low_back(v):
    return v

def low_keep(v):
    return (low(v), None)

def low_pass(kept, grad):
    return (grad,)

def back_keep(v):
    return (v, None)

def back_low(kept, grad):
    return (low(grad),)
low.defvjp(low_keep, low_pass)
low_back.defvjp(back_keep, back_low)

def rms_norm(value_matrix, gain):
    return value_matrix * lax.rsqrt(lax.optimization_barrier(jnp.mean(value_matrix * value_matrix, axis=-1, keepdims=True)) + EPS) * gain

def rotate(value_matrix, cosine_table, sine_table):
    half_dim = value_matrix.shape[-1] // 2
    first_half = value_matrix[..., :half_dim]
    second_half = value_matrix[..., half_dim:]
    return jnp.concatenate([first_half * cosine_table - second_half * sine_table, first_half * sine_table + second_half * cosine_table], axis=-1)

def layout(lengths):
    utter_ends = jnp.cumsum(lengths, axis=-1).astype(jnp.int32)
    starts = utter_ends - lengths
    places = jnp.arange(BIN, dtype=jnp.int32)
    segment = lax.optimization_barrier(jnp.sum((places[None, :, None] >= utter_ends[:, None, :]).astype(jnp.int32), axis=-1))
    member = segment[:, :, None] == jnp.arange(UTTS, dtype=jnp.int32)[None, None, :]
    offsets = lax.optimization_barrier(jnp.sum(jnp.where(member, starts[:, None, :], 0), axis=-1))
    position = places[None, :] - offsets
    frequency = 10000.0 ** (-jnp.arange(HD // 2, dtype=jnp.float32) * 2.0 / HD)
    angles = position.astype(jnp.float32)[..., None] * frequency
    return (segment, jnp.cos(angles)[:, :, None, :], jnp.sin(angles)[:, :, None, :])

def dispatch_tables(routes):
    chosen = routes[..., 0].reshape(BINS, N_HIDDEN, QF)
    onehot = (chosen[..., None] == jnp.arange(EXPERTS, dtype=jnp.int32)).astype(jnp.int32)
    running = jnp.cumsum(onehot, axis=2)
    slot_index = lax.optimization_barrier(jnp.sum((running - 1) * onehot, axis=-1))
    slot_table = onehot[..., None] * (slot_index[..., None, None] == jnp.arange(CAP, dtype=jnp.int32)).astype(jnp.int32)
    return (slot_table.astype(jnp.float32), onehot.reshape(BINS, BIN, EXPERTS).astype(jnp.float32))

def attend(inputs):
    queries, key_rows, value_rows, segment = inputs
    scores = low_back(jnp.einsum('qhe,khe->hqk', queries, key_rows, precision=BEST) * HD ** (-0.5))
    same_utter = segment[:, None] == segment[None, :]
    scores = jnp.where(same_utter[None], scores, NEG)
    weights = low(jax.nn.softmax(scores, axis=-1))
    return jnp.einsum('hqk,khe->qhe', weights, value_rows, precision=BEST)

def conformer_layer(residual_stream, masters, segment, cosine_table, sine_table, slot_table, onehot):
    entry_low = low(masters[0])
    exit_low = low(masters[1])
    upward_low = low(masters[2])
    downward_low = low(masters[3])
    gains = masters[4]
    kernel = masters[5]
    router_low = low(masters[6])
    normed = low(rms_norm(residual_stream, gains[0]))
    feedforward_inner = low_back(jnp.einsum('bfd,djc->bfjc', normed, entry_low[:, 0:4], precision=BEST))
    hidden = low(jax.nn.silu(feedforward_inner))
    branch = low_back(jnp.einsum('bfjc,jcd->bfd', hidden, exit_low[0:4], precision=BEST))
    encoding_following_pointwise = residual_stream + 0.5 * branch
    normed = low(rms_norm(encoding_following_pointwise, gains[1]))
    threefold_projection = low_back(jnp.einsum('bfd,djc->bfjc', normed, entry_low[:, 4:7], precision=BEST)).reshape(BINS, BIN, 3, HEADS, HD)
    queries = low(rotate(threefold_projection[:, :, 0], cosine_table, sine_table))
    key_rows = low(rotate(threefold_projection[:, :, 1], cosine_table, sine_table))
    value_rows = low(threefold_projection[:, :, 2])
    context = lax.map(jax.checkpoint(attend), (queries, key_rows, value_rows, segment))
    context = low(low_back(context)).reshape(BINS, BIN, D)
    branch = low_back(jnp.einsum('bfc,cd->bfd', context, exit_low[4], precision=BEST))
    after_attn = encoding_following_pointwise + branch
    normed = low(rms_norm(after_attn, gains[2]))
    gated_product = low_back(jnp.einsum('bfd,djc->bfjc', normed, entry_low[:, 7:9], precision=BEST))
    glu_low = low(gated_product[:, :, 0] * jax.nn.sigmoid(gated_product[:, :, 1]))
    conv_half = KER // 2
    padded = jnp.pad(glu_low, ((0, 0), (conv_half, conv_half), (0, 0)))
    padded_segment = jnp.pad(segment, ((0, 0), (conv_half, conv_half)), constant_values=-1)
    convolution_mixture = jnp.zeros_like(glu_low)
    for offset in range(KER):
        same_utter = (padded_segment[:, offset:offset + BIN] == segment)[..., None]
        convolution_mixture = convolution_mixture + kernel[offset] * jnp.where(same_utter, padded[:, offset:offset + BIN], 0.0)
    convolution_mixture = low_back(convolution_mixture)
    swish_activated = low(jax.nn.silu(convolution_mixture))
    branch = low_back(jnp.einsum('bfc,cd->bfd', swish_activated, exit_low[5], precision=BEST))
    after_conv = after_attn + branch
    normed = low(rms_norm(after_conv, gains[3]))
    logits = jnp.einsum('bfd,de->bfe', normed, router_low, precision=BEST)
    sigmoid_control_entries = lax.optimization_barrier(jnp.sum(jax.nn.softmax(logits, axis=-1) * onehot, axis=-1, keepdims=True))
    blocks = normed.reshape(BINS, N_HIDDEN, QF, D)
    sent = low_back(jnp.einsum('bhqec,bhqd->ebhcd', slot_table, blocks, precision=BEST))
    expert_inner = low_back(jnp.einsum('ebhcd,edf->ebhcf', sent, upward_low, precision=BEST))
    expert_hidden = low(jax.nn.silu(expert_inner))
    result = low(low_back(jnp.einsum('ebhcf,efd->ebhcd', expert_hidden, downward_low, precision=BEST)))
    mixture_backward = jnp.einsum('bhqec,ebhcd->bhqd', slot_table, result, precision=BEST).reshape(BINS, BIN, D)
    after_moe = after_conv + 0.5 * sigmoid_control_entries * mixture_backward
    return rms_norm(after_moe, gains[4])

def forward(inputs, masters, segment, cosine_table, sine_table, slot_table, onehot):
    residual_stream = inputs
    for layer_index in range(LAYERS):
        layer_masters = tuple((master[layer_index] for master in masters))
        residual_stream = conformer_layer(residual_stream, layer_masters, segment, cosine_table, sine_table, slot_table, onehot)
    return residual_stream

def adamw(master, moment, square, gradient, rate, decay):
    moment_new = BETA_ONE * moment + (1.0 - BETA_ONE) * gradient
    square_new = BETA_TWO * square + (1.0 - BETA_TWO) * gradient * gradient
    unbiased = moment_new / (1.0 - BETA_ONE ** STEP)
    scaled = square_new / (1.0 - BETA_TWO ** STEP)
    updated = master - rate * (unbiased / (jnp.sqrt(scaled) + ADAM_EPS) + decay * master)
    return (updated, moment_new, square_new)

def reference(frames, cotangent, lengths, routes, entry_weights, entry_moment, entry_square, exit_weights, exit_moment, exit_square, upward_weights, upward_moment, upward_square, downward_weights, downward_moment, downward_square, norm_gains, gains_moment, gains_square, conv_kernel, kernel_moment, kernel_square, router_weights, router_moment, router_square):
    segment, cosine_table, sine_table = layout(lengths)
    slot_table, onehot = dispatch_tables(routes)
    masters = (entry_weights, exit_weights, upward_weights, downward_weights, norm_gains, conv_kernel, router_weights)

    def run(inputs, weights):
        return forward(inputs, weights, segment, cosine_table, sine_table, slot_table, onehot)
    encoded, pullback = jax.vjp(run, frames.astype(jnp.float32), masters)
    input_gradient, gradients = pullback(cotangent.astype(jnp.float32))
    wide_rate = 2.0 * D ** (-0.5)
    entry_next = adamw(entry_weights, entry_moment, entry_square, gradients[0], wide_rate, DECAY)
    exit_next = adamw(exit_weights, exit_moment, exit_square, gradients[1], wide_rate, DECAY)
    upward_next = adamw(upward_weights, upward_moment, upward_square, gradients[2], wide_rate, DECAY)
    downward_next = adamw(downward_weights, downward_moment, downward_square, gradients[3], 2.0 * max(EFF // 64, 1) ** (-0.5), DECAY)
    gains_next = adamw(norm_gains, gains_moment, gains_square, gradients[4], 0.5, 0.0)
    kernel_next = adamw(conv_kernel, kernel_moment, kernel_square, gradients[5], 2.0 * KER ** (-0.5), DECAY)
    router_next = adamw(router_weights, router_moment, router_square, gradients[6], wide_rate, DECAY)
    return (encoded, input_gradient, entry_next[0], entry_next[1], entry_next[2], exit_next[0], exit_next[1], exit_next[2], upward_next[0], upward_next[1], upward_next[2], downward_next[0], downward_next[1], downward_next[2], gains_next[0], gains_next[1], gains_next[2], kernel_next[0], kernel_next[1], kernel_next[2], router_next[0], router_next[1], router_next[2])
```

```python
import functools
import math

import jax
import jax.numpy as jnp
import numpy as np
from jax import lax
from jax.experimental import pallas as pl
from jax.experimental.pallas import tpu as pltpu
from jax.sharding import Mesh
from jax.sharding import PartitionSpec as P

D = 512
HEADS = 8
HD = 64
HALF = HD // 2
EFF = 2048
EXPERTS = 8
KER = 15
RIM = KER // 2
LAYERS = 2
STEP = 5
EPS = 1e-05
NEG = -1e30
BETA_ONE = 0.9
BETA_TWO = 0.98
ADAM_EPS = 1e-08
DECAY = 0.01
BEST = lax.Precision.HIGHEST
F32 = jnp.float32
BF16 = jnp.bfloat16

DP, EB, ES, HX, HC = "dp", "eb", "es", "hx", "hc"
ALL = (DP, EB, ES, HX, HC)
EXPERT = (EB, ES)
PLANE = (DP, HX)
MOE = (EB, ES, HC)


def paired():
    return lax.axis_size(HC) == lax.axis_size(ES)


def frame_axes():
    return (HX, ES, HC) if paired() else (HX, HC, ES)


def sub_axis():
    return HC if paired() else ES


def dot(left, right, left_dim, right_dim, **kw):
    return lax.dot_general(
        left, right, (((left_dim,), (right_dim,)), ((), ())), preferred_element_type=F32, **kw
    )


def swap(block):
    return lax.ppermute(block, HC, [(0, 1), (1, 0)])


def take(block, axis, index):
    return lax.dynamic_index_in_dim(block, index, axis, keepdims=False)


def stack_pair(own, other, axis):
    me = lax.axis_index(HC)
    return jnp.where(
        me == 0, jnp.stack([own, other], axis), jnp.stack([other, own], axis)
    )


def exchange(block, axes):
    return lax.all_to_all(block, axes, split_axis=0, concat_axis=0, tiled=True)


def flipped():
    return paired() and lax.axis_size(PLANE) == 4 and lax.axis_size(EXPERT) == 4


def flip(block, axes, k):
    return lax.ppermute(block, axes, [(i, i ^ k) for i in range(lax.axis_size(axes))])


def tie(value, others):
    value, others = lax.optimization_barrier((value, tuple(others)))
    return value, list(others)


class Queue:
    def __init__(self):
        self.groups = []

    def add(self, arrays, then):
        self.groups.append((list(arrays), then))

    def join(self, arrays, then):
        arrays = list(arrays)
        if not self.groups:
            return self.add(arrays, then)
        count, (others, after) = len(arrays), self.groups[0]

        def both(got):
            then(got[:count])
            after(got[count:])

        self.groups[0] = (arrays + others, both)

    def point(self, value):
        if self.groups:
            arrays, then = self.groups.pop(0)
            value, arrays = tie(value, arrays)
            then(arrays)
        return value

    def flush(self):
        while self.groups:
            arrays, then = self.groups.pop(0)
            then(arrays)

    def add_pieces(self, pieces, then, sizes):
        got, at = [], 0
        for size in sizes:
            end = at + size if size else len(pieces)
            last = end >= len(pieces)

            def arrived(arrays, last=last):
                got.extend(arrays)
                if last:
                    then(got)

            if at < len(pieces):
                self.add(pieces[at:end], arrived)
            at = end


def passed(pieces, axes):
    if flipped():
        return [pieces[0]] + [flip(pieces[k], axes, k) for k in range(1, len(pieces))]
    whole = exchange(jnp.stack(pieces), axes)
    return [whole[k] for k in range(len(pieces))]


def summed(pieces):
    return functools.reduce(jnp.add, [p.astype(F32) for p in pieces])


def summed_everywhere(value, axes):
    for axis in axes:
        k = 1
        while k < lax.axis_size(axis):
            value = value + flip(value, axis, k)
            k *= 2
    return value


def to_frames(block):
    bins, rows, width = block.shape
    parts = lax.axis_size(sub_axis())
    block = block.reshape(bins, parts, rows // parts, width)
    if paired():
        me = lax.axis_index(HC)
        block = stack_pair(take(block, 1, me), swap(take(block, 1, 1 - me)), 1)
    block = exchange(block.reshape(bins * parts, rows // parts, width), EXPERT)
    return jnp.swapaxes(block, 0, 1).reshape(rows // parts, -1)


def from_frames(block):
    rows, width = block.shape
    groups, parts = lax.axis_size(EXPERT), lax.axis_size(sub_axis())
    bins = groups // parts
    block = jnp.swapaxes(block.reshape(rows, groups, width // groups), 0, 1)
    block = exchange(block, EXPERT).reshape(bins, parts, rows, width // groups)
    if paired():
        me = lax.axis_index(HC)
        block = stack_pair(take(block, 1, me), swap(take(block, 1, 1 - me)), 1)
    return block.reshape(bins, rows * parts, width // groups)


def spread(block):
    width = block.shape[1] // lax.axis_size(sub_axis())
    if paired():
        me = feature_part()
        own = lax.dynamic_slice_in_dim(block, me * width, width, axis=1)
        other = lax.dynamic_slice_in_dim(block, (1 - me) * width, width, axis=1)
        return jnp.concatenate([own, swap(other)], axis=0)
    return lax.all_to_all(block, ES, split_axis=1, concat_axis=0, tiled=True)


def feature_part():
    me = lax.axis_index(HC)
    return me ^ lax.axis_index(DP) if flipped() else me


def unspread(block):
    rows = block.shape[0] // 2
    if paired():
        own, other = block[:rows], swap(block[rows:])
        return jnp.where(
            feature_part() == 0,
            jnp.concatenate([own, other], axis=1),
            jnp.concatenate([other, own], axis=1),
        )
    return lax.all_to_all(block, ES, split_axis=0, concat_axis=1, tiled=True)


def dense_shard(entry, leave):
    entry = jnp.swapaxes(entry.astype(BF16), 0, 1)
    leave = jnp.swapaxes(leave.astype(BF16), 1, 2)
    return jnp.concatenate([entry, leave], axis=0)


def unpack_kernel(in_ref, *outs):
    _, groups, _, _, _, width = in_ref.shape
    at = 0
    for out in outs:
        for k in range(out.shape[1] // width):
            out[:, k * width : (k + 1) * width] = in_ref[0, k % groups, 0, at + k // groups]
        at += out.shape[1] // (width * groups)


def dense_gather(shard, units):
    count, rows, columns = shard.shape
    n_dp, n_e, n_h = lax.axis_size(DP), lax.axis_size(EXPERT), lax.axis_size((HX, HC))
    whole = lax.all_gather(shard, ALL, axis=0, tiled=False)
    whole = whole.reshape(n_dp, n_e, n_h, count, rows, columns)
    return pl.pallas_call(
        unpack_kernel,
        grid=(n_dp * n_h,),
        in_specs=[
            pl.BlockSpec(
                (1, n_e, 1, count, rows, columns), lambda r: (r // n_h, 0, r % n_h, 0, 0, 0)
            )
        ],
        out_specs=[pl.BlockSpec((rows, n * D), lambda r: (r, 0)) for n in units],
        out_shape=[jax.ShapeDtypeStruct((D, n * D), BF16) for n in units],
        compiler_params=pltpu.CompilerParams(vmem_limit_bytes=32 << 20),
        cost_estimate=pl.CostEstimate(
            flops=0, bytes_accessed=4 * count * D * D, transcendentals=0
        ),
    )(whole)


def pack_kernel(base, *refs):
    out = refs[-1]
    _, groups, _, _, width = out.shape
    at = 0
    for ref in refs[:-1]:
        for k in range(ref.shape[1] // width):
            out[0, (k % groups) ^ base[2], at + k // groups] = ref[:, k * width : (k + 1) * width]
        at += ref.shape[1] // (width * groups)


def dense_pack(grads, core):
    n_e, n_p, n_c = lax.axis_size(EXPERT), lax.axis_size(PLANE), lax.axis_size(HC)
    count = sum(g.shape[1] for g in grads) // D
    rows, columns = D // (n_p * n_c), D // n_e
    shape = (n_p, n_e, count, rows, columns)
    base = [core] + [lax.axis_index(a) if flipped() else 0 for a in (PLANE, EXPERT)]
    return pl.pallas_call(
        pack_kernel,
        grid_spec=pltpu.PrefetchScalarGridSpec(
            num_scalar_prefetch=1,
            grid=(n_p,),
            in_specs=[
                pl.BlockSpec((rows, g.shape[1]), lambda p, at: ((p ^ at[1]) * n_c + at[0], 0))
                for g in grads
            ],
            out_specs=pl.BlockSpec((1,) + shape[1:], lambda p, at: (p, 0, 0, 0, 0)),
        ),
        out_shape=jax.ShapeDtypeStruct(shape, BF16),
        compiler_params=pltpu.CompilerParams(vmem_limit_bytes=32 << 20),
        cost_estimate=pl.CostEstimate(
            flops=0, bytes_accessed=4 * count * D * D // n_c, transcendentals=0
        ),
    )(jnp.stack([jnp.asarray(b, jnp.int32) for b in base]), *grads)


def dense_pieces(grads):
    me = lax.axis_index(HC)
    own = dense_pack(grads, me)
    return [own] if lax.axis_size(HC) == 1 else [own, swap(dense_pack(grads, 1 - me))]


def dense_plane(pieces):
    parts = summed(pieces).astype(BF16)
    return passed([parts[k] for k in range(parts.shape[0])], PLANE)


def dense_expert(pieces):
    parts = summed(pieces).astype(BF16)
    return passed([parts[k] for k in range(parts.shape[0])], EXPERT)


def expert_gather(up, down):
    up, down = up.astype(BF16), down.astype(BF16)
    if lax.axis_size(HC) == 2:
        me = lax.axis_index(HC)
        up = jnp.concatenate([take(up, 0, me), swap(take(up, 0, 1 - me))], axis=1)
        down = jnp.concatenate([take(down, 0, me), swap(take(down, 0, 1 - me))], axis=0)
    else:
        up, down = up[0], down[0]
    count = lax.axis_size(PLANE)
    return passed([up] * count, PLANE) + passed([down] * count, PLANE)


EXPERT_STEPS = (3, 1, 3, 0)


def expert_scatter(pieces):
    count = len(pieces) // 2
    return passed(pieces[:count], PLANE) + passed(pieces[count:], PLANE)


def expert_sum(pieces):
    count = len(pieces) // 2
    up, down = summed(pieces[:count]), summed(pieces[count:])
    if lax.axis_size(HC) == 2:
        width = up.shape[1] // 2
        up = stack_pair(up[:, :width], swap(up[:, width:].astype(BF16)).astype(F32), 0)
        down = stack_pair(down[:width], swap(down[width:].astype(BF16)).astype(F32), 0)
        return up, down
    return up[None], down[None]


def gather_rows(in_ref, out, parts):
    _, capacity, width = in_ref.shape
    for i in range(in_ref.shape[0]):
        g, p = i // parts, i % parts
        out[g * capacity : (g + 1) * capacity, p * width : (p + 1) * width] = in_ref[i]


def part_rows(value, out_ref, parts):
    _, capacity, width = out_ref.shape
    for i in range(out_ref.shape[0]):
        g, p = i // parts, i % parts
        rows = value[g * capacity : (g + 1) * capacity, p * width : (p + 1) * width]
        out_ref[i] = rows.astype(out_ref.dtype)


def expert_kernel(parts, n_dp, x_ref, *refs):
    y_ref, x, y = refs[-3:]
    ups, downs = refs[: len(refs) // 2 - 1], refs[len(refs) // 2 - 1 : -3]
    depth, step = ups[0].shape[0], pl.program_id(0)

    @pl.when(step == 0)
    def _():
        gather_rows(x_ref, x, parts)
        y[...] = jnp.zeros_like(y)

    cuts = [slice(i * depth, (i + 1) * depth) for i in range(n_dp)]
    each = len(ups) // n_dp
    for n in range(each):
        u = sum(contract(x[:, cuts[i]], ups[i * each + n][...], 1, 0) for i in range(n_dp))
        hidden = (u * jax.nn.sigmoid(u)).astype(BF16)
        for i in range(n_dp):
            y[:, cuts[i]] += contract(hidden, downs[i * each + n][...], 1, 0)

    @pl.when(step == pl.num_programs(0) - 1)
    def _():
        part_rows(y[...], y_ref, parts)


def expert_back_kernel(parts, n_dp, x_ref, g_ref, *refs):
    x, g, dx = refs[-3:]
    count = (len(refs) - 4) // 4
    ups, downs = refs[:count], refs[count : 2 * count]
    dx_ref, dups, ddowns = refs[2 * count], refs[2 * count + 1 : -3 - count], refs[-3 - count : -3]
    depth, step = ups[0].shape[0], pl.program_id(0)

    @pl.when(step == 0)
    def _():
        gather_rows(x_ref, x, parts)
        gather_rows(g_ref, g, parts)
        dx[...] = jnp.zeros_like(dx)

    cuts = [slice(i * depth, (i + 1) * depth) for i in range(n_dp)]
    each = count // n_dp
    for n in range(each):
        at = [i * each + n for i in range(n_dp)]
        u = sum(contract(x[:, cuts[i]], ups[at[i]][...], 1, 0) for i in range(n_dp))
        logistic = jax.nn.sigmoid(u)
        hidden = (u * logistic).astype(BF16)
        dh = sum(contract(g[:, cuts[i]], downs[at[i]][...], 1, 1) for i in range(n_dp))
        du = (dh * (logistic * (1.0 + u * (1.0 - logistic)))).astype(BF16)
        for i in range(n_dp):
            dups[at[i]][...] = contract(x[:, cuts[i]], du, 0, 0).astype(BF16)
            ddowns[at[i]][...] = contract(hidden, g[:, cuts[i]], 0, 0).astype(BF16)
            dx[:, cuts[i]] += contract(du, ups[at[i]][...], 1, 1)

    @pl.when(step == pl.num_programs(0) - 1)
    def _():
        part_rows(dx[...], dx_ref, parts)


def expert_call(pieces, weights, grads=None):
    parts = D // pieces.shape[2]
    n_dp = lax.axis_size(DP)
    depth, width = weights[0].shape
    cut = min(width, 512)
    rows = pieces.size // D
    whole = pl.BlockSpec(pieces.shape, lambda c: (0, 0, 0))
    count = len(weights) // 2
    slabs = [pl.BlockSpec((depth, cut), lambda c: (0, c))] * count
    slabs += [pl.BlockSpec((cut, depth), lambda c: (c, 0))] * count
    shape = jax.ShapeDtypeStruct(pieces.shape, BF16)
    kept = pltpu.VMEM((rows, D), BF16)
    if grads is None:
        return pl.pallas_call(
            functools.partial(expert_kernel, parts, n_dp),
            grid=(width // cut,),
            in_specs=[whole] + slabs,
            out_specs=whole,
            out_shape=shape,
            scratch_shapes=[kept, pltpu.VMEM((rows, D), F32)],
            compiler_params=pltpu.CompilerParams(vmem_limit_bytes=40 << 20),
            cost_estimate=pl.CostEstimate(
                flops=4 * rows * D * EFF, bytes_accessed=4 * D * EFF, transcendentals=rows * EFF
            ),
        )(pieces, *weights)
    out = pl.pallas_call(
        functools.partial(expert_back_kernel, parts, n_dp),
        grid=(width // cut,),
        in_specs=[whole, whole] + slabs,
        out_specs=[whole] + slabs,
        out_shape=[shape] + [jax.ShapeDtypeStruct(w.shape, BF16) for w in weights],
        scratch_shapes=[kept, kept, pltpu.VMEM((rows, D), F32)],
        compiler_params=pltpu.CompilerParams(vmem_limit_bytes=40 << 20),
        cost_estimate=pl.CostEstimate(
            flops=12 * rows * D * EFF, bytes_accessed=8 * D * EFF, transcendentals=rows * EFF
        ),
    )(pieces, grads, *weights)
    return out[0], out[1:]


def swish_derivative(value):
    logistic = jax.nn.sigmoid(value)
    return logistic * (1.0 + value * (1.0 - logistic))


def norm_forward(value, gain):
    factor = lax.rsqrt(jnp.mean(value * value, axis=-1, keepdims=True) + EPS)
    return value * factor * gain, factor


def norm_backward(upstream, value, factor, gain):
    gain_grad = jnp.sum(upstream * value * factor, axis=0)
    scaled = gain * upstream
    mixed = jnp.sum(scaled * value, axis=-1, keepdims=True)
    return factor * scaled - value * (factor**3 * mixed / D), gain_grad


def rotate(value, cosine, sine):
    low, high = value[..., :HALF, :], value[..., HALF:, :]
    return jnp.concatenate([low * cosine - high * sine, low * sine + high * cosine], axis=-2)


def unrotate(value, cosine, sine):
    low, high = value[..., :HALF, :], value[..., HALF:, :]
    return jnp.concatenate([low * cosine + high * sine, high * cosine - low * sine], axis=-2)


def contract(left, right, left_dim, right_dim):
    return lax.dot_general(
        left, right, (((left_dim,), (right_dim,)), ((), ())), preferred_element_type=F32
    )


def masked_scores(key, query, low, high, base):
    raw = contract(key, query, 0, 0)
    place = base + lax.broadcasted_iota(jnp.int32, raw.shape, 0)
    return jnp.where((place >= low) & (place < high), raw, NEG)


def attend_kernel(span_ref, q_ref, k_ref, v_ref, o_ref, lse_ref, scores):
    count, width = k_ref.shape[0], k_ref.shape[-1]
    low, high = span_ref[0, 0:1], span_ref[0, 1:2]
    query = q_ref[0, 0, 0]
    peak = None
    for i in range(count):
        part = masked_scores(k_ref[i, 0, 0], query, low, high, i * width)
        scores[i] = part
        top = jnp.max(part, axis=0, keepdims=True)
        peak = top if peak is None else jnp.maximum(peak, top)
    total = jnp.zeros_like(peak)
    for i in range(count):
        part = jnp.exp(scores[i] - peak)
        scores[i] = part
        total = total + jnp.sum(part, axis=0, keepdims=True)
    inverse = 1.0 / total
    mixed = jnp.zeros(query.shape, F32)
    for i in range(count):
        mixed = mixed + contract(v_ref[i, 0, 0], (scores[i] * inverse).astype(BF16), 1, 0)
    o_ref[0, 0] = mixed.astype(BF16)
    lse_ref[0, 0] = peak + jnp.log(total)


def attend_back_kernel(
    span_ref, rot_q, rot_k, q_ref, k_ref, v_ref, g_ref, lse_ref, dq_ref, dkv_ref, dk, dv, probs, dots
):
    count, width = k_ref.shape[0], k_ref.shape[-1]
    step, last = pl.program_id(1), pl.num_programs(1) - 1
    low, high = span_ref[0, 0:1], span_ref[0, 1:2]
    query, grad, log_total = q_ref[0, 0, 0], g_ref[0, 0], lse_ref[0, 0]

    @pl.when(step == 0)
    def _():
        dk[...] = jnp.zeros_like(dk)
        dv[...] = jnp.zeros_like(dv)

    delta = jnp.zeros_like(log_total)
    for i in range(count):
        part = jnp.exp(masked_scores(k_ref[i, 0, 0], query, low, high, i * width) - log_total)
        probs[i] = part
        dots[i] = contract(v_ref[i, 0, 0], grad, 0, 0)
        delta = delta + jnp.sum(part * dots[i], axis=0, keepdims=True)
    dq = jnp.zeros(query.shape, F32)
    for i in range(count):
        part = probs[i]
        slope = (part * (dots[i] - delta)).astype(BF16)
        dv[i] += contract(grad, part.astype(BF16), 1, 1)
        dk[i] += contract(query, slope, 1, 1)
        dq = dq + contract(k_ref[i, 0, 0], slope, 1, 0)
    dq_ref[0, 0] = unrotate(dq * HD ** (-0.5), rot_q[0, 0], rot_q[0, 1]).astype(BF16)

    @pl.when(step == last)
    def _():
        for i in range(count):
            dkv_ref[i, 0, 0] = unrotate(dk[i], rot_k[i, 0], rot_k[i, 1]).astype(BF16)
            dkv_ref[i, 1, 0] = dv[i].astype(BF16)


def attend(spans, queries, keys, first):
    nq, _, heads, _, width = queries.shape
    nk = keys.shape[0]
    side = lambda at: pl.BlockSpec((nk, 1, 1, HD, width), lambda h, j: (0, at, h, 0, 0))
    return pl.pallas_call(
        attend_kernel,
        grid=(heads, nq),
        in_specs=[
            pl.BlockSpec((1, 2, width), lambda h, j: (j, 0, 0)),
            pl.BlockSpec((1, 1, 1, HD, width), lambda h, j: (j, 0, h, 0, 0)),
            side(first),
            side(first + 1),
        ],
        out_specs=[
            pl.BlockSpec((1, 1, HD, width), lambda h, j: (j, h, 0, 0)),
            pl.BlockSpec((1, 1, 1, width), lambda h, j: (j, h, 0, 0)),
        ],
        out_shape=[
            jax.ShapeDtypeStruct((nq, heads, HD, width), BF16),
            jax.ShapeDtypeStruct((nq, heads, 1, width), F32),
        ],
        scratch_shapes=[pltpu.VMEM((nk, width, width), F32)],
        compiler_params=pltpu.CompilerParams(vmem_limit_bytes=40 << 20),
        cost_estimate=pl.CostEstimate(
            flops=4 * heads * nq * nk * width * width * HD,
            bytes_accessed=4 * heads * (nq + nk) * HD * width,
            transcendentals=heads * nq * nk * width * width,
        ),
    )(spans, queries, keys, keys)


def attend_back(spans, rot_q, rot_k, queries, keys, first, grads, log_total):
    nq, _, heads, _, width = queries.shape
    nk = keys.shape[0]
    side = lambda at: pl.BlockSpec((nk, 1, 1, HD, width), lambda h, j: (0, at, h, 0, 0))
    return pl.pallas_call(
        attend_back_kernel,
        grid=(heads, nq),
        in_specs=[
            pl.BlockSpec((1, 2, width), lambda h, j: (j, 0, 0)),
            pl.BlockSpec((1, 2, HALF, width), lambda h, j: (j, 0, 0, 0)),
            pl.BlockSpec((nk, 2, HALF, width), lambda h, j: (0, 0, 0, 0)),
            pl.BlockSpec((1, 1, 1, HD, width), lambda h, j: (j, 0, h, 0, 0)),
            side(first),
            side(first + 1),
            pl.BlockSpec((1, 1, HD, width), lambda h, j: (j, h, 0, 0)),
            pl.BlockSpec((1, 1, 1, width), lambda h, j: (j, h, 0, 0)),
        ],
        out_specs=[
            pl.BlockSpec((1, 1, HD, width), lambda h, j: (j, h, 0, 0)),
            pl.BlockSpec((nk, 2, 1, HD, width), lambda h, j: (0, 0, h, 0, 0)),
        ],
        out_shape=[
            jax.ShapeDtypeStruct((nq, heads, HD, width), BF16),
            jax.ShapeDtypeStruct((nk, 2, heads, HD, width), BF16),
        ],
        scratch_shapes=[
            pltpu.VMEM((nk, HD, width), F32),
            pltpu.VMEM((nk, HD, width), F32),
            pltpu.VMEM((nk, width, width), F32),
            pltpu.VMEM((nk, width, width), F32),
        ],
        compiler_params=pltpu.CompilerParams(vmem_limit_bytes=40 << 20),
        cost_estimate=pl.CostEstimate(
            flops=10 * heads * nq * nk * width * width * HD,
            bytes_accessed=8 * heads * (nq + nk) * HD * width,
            transcendentals=heads * nq * nk * width * width,
        ),
    )(spans, rot_q, rot_k, queries, keys, keys, grads, log_total)


def build_tables(lengths, routes, rows):
    axes = frame_axes()
    total = rows * lax.axis_size(axes)
    order = lax.axis_index(axes)
    lengths = take(lengths, 0, lax.axis_index(EB))
    ends = jnp.cumsum(lengths)
    starts = ends - lengths
    places = jnp.arange(total, dtype=jnp.int32)
    segment = jnp.sum((places[:, None] >= ends[None, :]).astype(jnp.int32), axis=-1)
    member = segment[:, None] == jnp.arange(lengths.shape[0], dtype=jnp.int32)
    low = jnp.sum(jnp.where(member, starts, 0), axis=-1)
    high = jnp.sum(jnp.where(member, ends, 0), axis=-1)
    spans = jnp.stack([low, high]).reshape(2, -1, rows).swapaxes(0, 1)
    position = (places - low).reshape(-1, 1, rows)
    frequency = 10000.0 ** (-jnp.arange(HALF, dtype=F32) * 2.0 / HD)
    angles = position.astype(F32) * frequency[:, None]
    rotary = jnp.stack([jnp.cos(angles), jnp.sin(angles)], axis=1)
    wide = jnp.pad(segment, (RIM, RIM), constant_values=-1)
    wide = lax.dynamic_slice_in_dim(wide, order * rows, rows + 2 * RIM)
    own = wide[RIM : RIM + rows]
    masks = [(wide[i : i + rows] == own).astype(F32)[:, None] for i in range(KER)]

    routes = routes[..., 0]
    if paired():
        mine = lax.axis_index(HC) == lax.axis_index(ES)
        other = swap(routes)
        routes = jnp.where(mine, routes, other)
    chosen = take(routes, 0, lax.axis_index(EB))
    block = chosen.shape[0]
    capacity = 3 * block // 16
    experts = jnp.arange(EXPERTS, dtype=jnp.int32)
    onehot = chosen[:, None] == experts
    earlier = jnp.tril(jnp.ones((block, block), BF16), -1)
    slots = jnp.sum(jnp.where(onehot, dot(earlier, onehot.astype(BF16), 1, 0), 0.0), axis=-1)
    slots = slots.astype(jnp.int32)
    parts = lax.axis_size(sub_axis())
    sub = lax.axis_index(sub_axis())
    own_chosen = take(chosen.reshape(parts, -1), 0, sub)
    if paired():
        flip = lambda v: jnp.where(sub == 0, v, jnp.roll(v, block // 2))
        chosen, slots = flip(chosen), flip(slots)
    place = chosen * capacity + slots
    table = (jnp.arange(EXPERTS * capacity, dtype=jnp.int32)[:, None] == place).astype(BF16)
    own_onehot = (own_chosen[:, None] == experts).astype(F32)
    return spans, rotary, take(rotary, 0, order), take(spans, 0, order), masks, table, own_onehot


def rimmed(block):
    axes = (ES, HX, HC)
    sizes = [lax.axis_size(axis) for axis in axes]
    order = np.arange(math.prod(sizes)).reshape(sizes)
    order = [int(i) for i in np.transpose(order, [axes.index(a) for a in frame_axes()]).flat]
    low = lax.ppermute(block[-RIM:], axes, list(zip(order[:-1], order[1:])))
    high = lax.ppermute(block[:RIM], axes, list(zip(order[1:], order[:-1])))
    return jnp.concatenate([low, block, high], axis=0)


def to_experts(block, table):
    sent = dot(table, spread(block), 1, 0).astype(BF16)
    return exchange(sent.reshape(EXPERTS, -1, sent.shape[1]), MOE)


def from_experts(pieces, table):
    got = exchange(pieces, MOE).reshape(table.shape[0], -1)
    return unspread(dot(table, got, 0, 0).astype(BF16)).astype(F32)


def heads_apart(block):
    if lax.axis_size(frame_axes()) == HEADS:
        got = exchange(jnp.swapaxes(block, 0, 1), frame_axes())[:, :, None]
        return got, got, 1
    return block[None, :1], lax.all_gather(block[1:], frame_axes(), axis=0, tiled=False), 0


def heads_together(block):
    if lax.axis_size(frame_axes()) == HEADS:
        block = exchange(block, frame_axes())
    return block.reshape(HEADS * HD, -1)


def heads_grad(block):
    block = block.reshape(HEADS, HD, -1)
    if lax.axis_size(frame_axes()) == HEADS:
        return exchange(block, frame_axes())[:, None]
    return block[None]


def heads_back(dq, dkv):
    if lax.axis_size(frame_axes()) == HEADS:
        both = jnp.concatenate([dq[:, None], dkv], axis=1)[:, :, 0]
        both = jnp.swapaxes(exchange(both, frame_axes()), 0, 1)
    else:
        dkv = lax.psum_scatter(dkv, frame_axes(), scatter_dimension=0, tiled=False)
        both = jnp.concatenate([dq, dkv], axis=0)
    return both.reshape(3 * HEADS * HD, -1)


def forward_layer(x, weights, tables, queue):
    ffn_in, qkv, glu, ffn_out, attn_out, conv_out, expert, gains, kernel, router = weights
    spans, rotary, own_rotary, own_spans, masks, table, onehot = tables
    rows = x.shape[0]
    normed, r0 = norm_forward(x, gains[0])
    a0 = queue.point(normed.astype(BF16))
    u0 = dot(a0, ffn_in, 1, 0)
    h0 = jax.nn.silu(u0).astype(BF16)
    x1 = x + 0.5 * dot(h0, ffn_out, 1, 1)

    normed, r1 = norm_forward(x1, gains[1])
    a1 = normed.astype(BF16)
    t1 = dot(qkv, a1, 0, 1).reshape(3, HEADS, HD, rows)
    turned = rotate(t1[:2], own_rotary[0], own_rotary[1])
    query = (turned[0] * HD ** (-0.5)).astype(BF16)
    mixed = jnp.stack([query, turned[1].astype(BF16), t1[2].astype(BF16)])
    queries, keys, first = heads_apart(mixed)
    query_spans = spans if queries.shape[0] > 1 else own_spans[None]
    context, log_total = attend(query_spans, queries, keys, first)
    context = queue.point(context)
    o = heads_together(context)
    x2 = x1 + dot(o, attn_out, 0, 1)
    x2 = queue.point(x2)

    normed, r2 = norm_forward(x2, gains[2])
    a2 = normed.astype(BF16)
    g = dot(a2, glu, 1, 0)
    g0, logistic = g[:, :D], jax.nn.sigmoid(g[:, D:])
    z = rimmed((g0 * logistic).astype(BF16))
    wide = z.astype(F32)
    c = jnp.zeros((rows, D), F32)
    for i in range(KER):
        c = c + kernel[i] * (wide[i : i + rows] * masks[i])
    e = queue.point(jax.nn.silu(c).astype(BF16))
    x3 = x2 + dot(e, conv_out, 1, 1)

    normed, r3 = norm_forward(x3, gains[3])
    a3 = normed.astype(BF16)
    probs = jax.nn.softmax(dot(a3, router, 1, 1), axis=-1)
    gate = jnp.sum(probs * onehot, axis=-1, keepdims=True)
    sent = to_experts(a3, table)
    back = from_experts(queue.point(expert_call(sent, expert)), table)
    x4 = x3 + 0.5 * gate * back
    out, r4 = norm_forward(x4, gains[4])
    saved = (
        (x, r0, a0, u0, h0),
        (x1, r1, a1, queries, keys, log_total, o),
        (x2, r2, a2, g0, logistic, z, c, e),
        (x3, r3, a3, probs, gate, sent, back),
        (x4, r4),
    )
    return out, saved


def backward_layer(upstream, weights, saved, tables, queue, alone):
    ffn_in, qkv, glu, ffn_out, attn_out, conv_out, expert, gains, kernel, router = weights
    spans, rotary, own_rotary, own_spans, masks, table, onehot = tables
    rows = upstream.shape[0]
    x4, r4 = saved[4]
    dx4, dg4 = norm_backward(upstream, x4, r4, gains[4])

    x3, r3, a3, probs, gate, sent, back = saved[3]
    half = 0.5 * dx4
    dgate = jnp.sum(half * back, axis=-1, keepdims=True)
    dy = to_experts(queue.point((gate * half).astype(BF16)), table)
    dsent, dexpert = expert_call(sent, expert, queue.point(dy))
    total = []
    queue.add_pieces(
        expert_scatter(dexpert), lambda arrays: total.extend(expert_sum(arrays)), EXPERT_STEPS
    )
    dlogits = dgate * probs * (onehot - gate)
    da3 = from_experts(dsent, table) + dot(
        dlogits, router.astype(F32), 1, 0, precision=BEST
    )
    drouter = dot(dlogits, a3.astype(F32), 0, 0, precision=BEST)
    dn, dg3 = norm_backward(da3, x3, r3, gains[3])
    dx3 = dx4 + dn
    dx3 = queue.point(dx3)

    x2, r2, a2, g0, logistic, z, c, e = saved[2]
    dy2 = dx3.astype(BF16)
    dconv_out = dot(dy2, e, 0, 0).astype(BF16)
    dc = (dot(dy2, conv_out, 1, 0) * swish_derivative(c)).astype(BF16)
    dc = queue.point(dc)
    dc_wide = rimmed(dc).astype(F32)
    dc_own, wide = dc.astype(F32), z.astype(F32)
    dz = jnp.zeros((rows, D), F32)
    kernel_rows = []
    for i in range(KER):
        kernel_rows.append(jnp.sum(dc_own * (wide[i : i + rows] * masks[i]), axis=0))
        mirror = KER - 1 - i
        dz = dz + kernel[i] * (dc_wide[mirror : mirror + rows] * masks[mirror])
    dglu = jnp.concatenate(
        [dz * logistic, dz * g0 * logistic * (1.0 - logistic)], axis=1
    ).astype(BF16)
    dglu_in = dot(a2, dglu, 0, 0).astype(BF16)
    dn, dg2 = norm_backward(dot(dglu, glu, 1, 1), x2, r2, gains[2])
    dx2 = dx3 + dn

    x1, r1, a1, queries, keys, log_total, o = saved[1]
    dy1 = dx2.astype(BF16)
    dattn_out = dot(dy1, o, 0, 1).astype(BF16)
    grads = queue.point(heads_grad(dot(attn_out, dy1, 0, 1).astype(BF16)))
    many = queries.shape[0] > 1
    dq, dkv = attend_back(
        spans if many else own_spans[None],
        rotary if many else own_rotary[None],
        rotary,
        queries,
        keys,
        1 if many else 0,
        grads,
        log_total,
    )
    dt = heads_back(queue.point(dq), dkv)
    dqkv = dot(a1, dt, 0, 1).astype(BF16)
    dn, dg1 = norm_backward(dot(dt, qkv, 0, 1), x1, r1, gains[1])
    dx1 = dx2 + dn
    rest = [dqkv, dglu_in, dattn_out, dconv_out]
    if alone:
        rest = dense_pieces(rest)
    dx1 = queue.point(dx1)

    x0, r0, a0, u0, h0 = saved[0]
    dy0 = (0.5 * dx1).astype(BF16)
    dffn_out = dot(dy0, h0, 0, 0).astype(BF16)
    du0 = (dot(dy0, ffn_out, 1, 0) * swish_derivative(u0)).astype(BF16)
    dffn_in = dot(a0, du0, 0, 0).astype(BF16)
    dn, dg0 = norm_backward(dot(du0, ffn_in, 1, 1), x0, r0, gains[0])
    dx = dx1 + dn
    ffn = dense_pieces([dffn_in, dffn_out] + ([] if alone else rest))
    small = jnp.concatenate(
        [jnp.stack([dg0, dg1, dg2, dg3, dg4] + kernel_rows), drouter], axis=0
    )
    return dx, ffn, rest, total, small


def small_total(grad):
    groups = lax.axis_size(EXPERT)
    width = D // groups
    me = lax.axis_index(EXPERT)
    if flipped():
        pieces = [
            lax.dynamic_slice_in_dim(grad, (me ^ k) * width, width, axis=1) for k in range(groups)
        ]
    else:
        pieces = [grad[:, k * width : (k + 1) * width] for k in range(groups)]
    return summed_everywhere(summed(passed(pieces, EXPERT)), (HC, HX, DP))


def dense_order(*groups):
    if len(groups) == 1:
        both = summed(groups[0])
        ffn, rest = both[:8], both[8:]
    else:
        ffn, rest = summed(groups[0]), summed(groups[1])
    return jnp.concatenate([ffn[:4], rest[:5], ffn[4:], rest[5:]], axis=0)


def adamw(master, moment, square, gradient, rate, decay):
    moment_new = BETA_ONE * moment + (1.0 - BETA_ONE) * gradient
    square_new = BETA_TWO * square + (1.0 - BETA_TWO) * gradient * gradient
    unbiased = moment_new / (1.0 - BETA_ONE**STEP)
    scaled = square_new / (1.0 - BETA_TWO**STEP)
    updated = master - rate * (unbiased / (jnp.sqrt(scaled) + ADAM_EPS) + decay * master)
    return (updated, moment_new, square_new)


def on_device(
    frames,
    cotangent,
    lengths,
    routes,
    entry_weights,
    entry_moment,
    entry_square,
    exit_weights,
    exit_moment,
    exit_square,
    upward_weights,
    upward_moment,
    upward_square,
    downward_weights,
    downward_moment,
    downward_square,
    norm_gains,
    gains_moment,
    gains_square,
    conv_kernel,
    kernel_moment,
    kernel_square,
    router_weights,
    router_moment,
    router_square,
):
    small = jnp.concatenate(
        [norm_gains, conv_kernel, jnp.swapaxes(router_weights, 1, 2)], axis=1
    )
    small = lax.all_gather(small, EXPERT, axis=2, tiled=True)
    counts = (norm_gains.shape[1], conv_kernel.shape[1])
    x = to_frames(frames).astype(F32)
    upstream = to_frames(cotangent).astype(F32)
    tables = build_tables(lengths, routes, x.shape[0])
    dense_weights, expert_weights = [], []
    for l in range(LAYERS):
        shard = dense_shard(entry_weights[l], exit_weights[l])
        dense_weights.append(dense_gather(shard, (4, 3, 2, 4, 1, 1)))
        expert_weights.append(expert_gather(upward_weights[l], downward_weights[l]))
    queue = Queue()
    experts = [[] for _ in range(LAYERS)]
    for l in range(LAYERS):
        queue.add_pieces(expert_weights[l], experts[l].extend, EXPERT_STEPS)
    saved, layer_weights = [], []
    for l in range(LAYERS):
        weights = tuple(dense_weights[l]) + (
            experts[l],
            small[l, : counts[0]],
            small[l, counts[0] : sum(counts)],
            small[l, sum(counts) :].astype(BF16),
        )
        layer_weights.append(weights)
        x, kept = forward_layer(x, weights, tables, queue)
        saved.append(kept)
    queue.flush()
    encoded = from_frames(x.astype(BF16)).astype(F32)
    dense_grads, expert_grads, small_grads = [None] * LAYERS, [], []

    def scatter(l, pieces):
        def last(arrays):
            dense_grads[l] = dense_order(arrays)

        def middle(arrays):
            queue.join(dense_expert(arrays), last)

        def first(arrays):
            queue.add_pieces(dense_plane(arrays), middle, (3, 0))

        queue.add(pieces, first)

    for l in reversed(range(LAYERS)):
        upstream, ffn, rest, expert, small_grad = backward_layer(
            upstream, layer_weights[l], saved[l], tables, queue, l == 0
        )
        if l > 0:
            scatter(l, ffn)
        expert_grads.insert(0, expert)
        small_grads.insert(0, small_total(small_grad))
    dense_grads[0] = dense_order(dense_expert(dense_plane(ffn)), dense_expert(dense_plane(rest)))
    queue.flush()
    input_gradient = from_frames(upstream.astype(BF16)).astype(F32)

    dense_grad = jnp.stack(dense_grads)
    entry_grad = jnp.swapaxes(dense_grad[:, 0:9], 1, 2)
    exit_grad = jnp.swapaxes(dense_grad[:, 9:], 2, 3)
    upward_grad = jnp.stack([g[0] for g in expert_grads])
    downward_grad = jnp.stack([g[1] for g in expert_grads])
    small_grad = jnp.stack(small_grads)
    gains_grad = small_grad[:, : counts[0]]
    kernel_grad = small_grad[:, counts[0] : sum(counts)]
    router_grad = jnp.swapaxes(small_grad[:, sum(counts) :], 1, 2)

    wide_rate = 2.0 * D ** (-0.5)
    down_rate = 2.0 * max(EFF // 64, 1) ** (-0.5)
    kernel_rate = 2.0 * KER ** (-0.5)
    return (
        (encoded, input_gradient)
        + adamw(entry_weights, entry_moment, entry_square, entry_grad, wide_rate, DECAY)
        + adamw(exit_weights, exit_moment, exit_square, exit_grad, wide_rate, DECAY)
        + adamw(upward_weights, upward_moment, upward_square, upward_grad, wide_rate, DECAY)
        + adamw(downward_weights, downward_moment, downward_square, downward_grad, down_rate, DECAY)
        + adamw(norm_gains, gains_moment, gains_square, gains_grad, 0.5, 0.0)
        + adamw(conv_kernel, kernel_moment, kernel_square, kernel_grad, kernel_rate, DECAY)
        + adamw(router_weights, router_moment, router_square, router_grad, wide_rate, DECAY)
    )


def finer(mesh, bins):
    n_dp, n_expert, n_hidden = mesh.devices.shape
    each = bins // n_dp
    pair = EXPERTS // n_expert
    shape = (n_dp, each, n_expert // each, n_hidden // pair, pair)
    return Mesh(mesh.devices.reshape(shape), ALL)


def solution(mesh):
    hidden = (HX, HC)
    stream = P(DP, hidden, EXPERT)
    entry = P(None, (DP, HX, HC), None, EXPERT)
    leave = P(None, None, EXPERT, (DP, HX, HC))
    upward = P(None, EXPERT, DP, hidden)
    downward = P(None, EXPERT, hidden, DP)
    last = P(None, None, EXPERT)
    middle = P(None, EXPERT, None)
    states = sum([(s,) * 3 for s in (entry, leave, upward, downward, last, last, middle)], ())

    def program(*args):
        return jax.shard_map(
            on_device,
            mesh=finer(mesh, args[0].shape[0]),
            in_specs=(stream, stream, P(DP, None), P(DP, hidden, None)) + states,
            out_specs=(stream, stream) + states,
            check_vma=False,
        )(*args)

    return program
```

```python
import functools
import math

import jax
import jax.numpy as jnp
import numpy as np
from jax import lax
from jax.experimental import pallas as pl
from jax.experimental.pallas import tpu as pltpu
from jax.sharding import Mesh
from jax.sharding import PartitionSpec as P

D = 512
HEADS = 8
HD = 64
HALF = HD // 2
EFF = 2048
EXPERTS = 8
KER = 15
RIM = KER // 2
EDGE = 16
LARGE = 700 << 10
UNITS = (4, 3, 2, 4, 1, 1)
LAYERS = 2
STEP = 5
EPS = 1e-05
NEG = -1e30
BETA_ONE = 0.9
BETA_TWO = 0.98
ADAM_EPS = 1e-08
DECAY = 0.01
BEST = lax.Precision.HIGHEST
F32 = jnp.float32
BF16 = jnp.bfloat16

DP, EB, ES, HX, HC = "dp", "eb", "es", "hx", "hc"
ALL = (DP, EB, ES, HX, HC)
EXPERT = (EB, ES)
PLANE = (DP, HX)
MOE = (EB, ES, HC)


def paired():
    return lax.axis_size(HC) == lax.axis_size(ES)


def frame_axes():
    return (HX, ES, HC) if paired() else (HX, HC, ES)


def sub_axis():
    return HC if paired() else ES


def dot(left, right, left_dim, right_dim, **kw):
    return lax.dot_general(
        left, right, (((left_dim,), (right_dim,)), ((), ())), preferred_element_type=F32, **kw
    )


def swap(block):
    return lax.ppermute(block, HC, [(0, 1), (1, 0)])


def still(block):
    if block.size * block.dtype.itemsize < LARGE:
        return block
    return pltpu.with_memory_space_constraint(block, pltpu.HBM)


def shaped(shape, dtype):
    if math.prod(shape) * jnp.dtype(dtype).itemsize < LARGE:
        return jax.ShapeDtypeStruct(shape, dtype)
    return pltpu.HBM(shape, dtype)


def take(block, axis, index):
    return lax.dynamic_index_in_dim(block, index, axis, keepdims=False)


def stack_pair(own, other, axis):
    me = lax.axis_index(HC)
    return jnp.where(
        me == 0, jnp.stack([own, other], axis), jnp.stack([other, own], axis)
    )


def exchange(block, axes):
    return lax.all_to_all(block, axes, split_axis=0, concat_axis=0, tiled=True)


def flipped():
    return paired() and lax.axis_size(PLANE) == 4 and lax.axis_size(EXPERT) == 4


def flip(block, axes, k):
    return lax.ppermute(block, axes, [(i, i ^ k) for i in range(lax.axis_size(axes))])


def tie(value, others):
    value, others = lax.optimization_barrier((value, tuple(others)))
    return value, list(others)


class Queue:
    def __init__(self):
        self.marks = {}

    def at(self, mark, arrays, then):
        self.marks.setdefault(mark, []).append((list(arrays), then))

    def point(self, mark, value):
        for arrays, then in self.marks.pop(mark, []):
            value, arrays = tie(value, arrays)
            then(arrays)
        return value


def passed(pieces, axes):
    if flipped():
        return [pieces[0]] + [flip(pieces[k], axes, k) for k in range(1, len(pieces))]
    whole = exchange(jnp.stack(pieces) if isinstance(pieces, list) else pieces, axes)
    return [whole[k] for k in range(whole.shape[0])]


def summed(pieces):
    return functools.reduce(jnp.add, [p.astype(F32) for p in pieces])


def summed_everywhere(value, axes):
    for axis in axes:
        k = 1
        while k < lax.axis_size(axis):
            value = value + flip(value, axis, k)
            k *= 2
    return value


def to_frames(block):
    bins, rows, width = block.shape
    parts = lax.axis_size(sub_axis())
    block = block.reshape(bins, parts, rows // parts, width)
    if paired():
        me = lax.axis_index(HC)
        block = stack_pair(take(block, 1, me), swap(take(block, 1, 1 - me)), 1)
    block = exchange(block.reshape(bins * parts, rows // parts, width), EXPERT)
    return jnp.swapaxes(block, 0, 1).reshape(rows // parts, -1)


def from_frames(block):
    groups, parts = lax.axis_size(EXPERT), lax.axis_size(sub_axis())
    bins, width = groups // parts, D // groups
    runs = 2
    rows = block.shape[0] // runs
    block = jnp.swapaxes(block.reshape(runs * rows, groups, width), 0, 1)
    block = exchange(block, EXPERT).reshape(bins, parts, runs, rows, width)
    if paired():
        me = lax.axis_index(HC)
        block = stack_pair(take(block, 1, me), swap(take(block, 1, 1 - me)), 2)
    else:
        block = jnp.swapaxes(block, 1, 2)
    return block.reshape(bins, runs * parts * rows, width)


def feature_part(turned):
    me = lax.axis_index(HC)
    return me ^ lax.axis_index(DP) if turned else me


def dense_shard(entry, leave):
    entry = jnp.swapaxes(entry.astype(BF16), 0, 1)
    leave = jnp.swapaxes(leave.astype(BF16), 1, 2)
    return jnp.concatenate([entry, leave], axis=0)


def unpack_kernel(in_ref, *outs):
    _, groups, _, _, _, width = in_ref.shape
    at = 0
    for out in outs:
        for k in range(out.shape[1] // width):
            out[:, k * width : (k + 1) * width] = in_ref[0, k % groups, 0, at + k // groups]
        at += out.shape[1] // (width * groups)


def dense_gather(shard, units):
    count, rows, columns = shard.shape
    n_dp, n_e, n_h = lax.axis_size(DP), lax.axis_size(EXPERT), lax.axis_size((HX, HC))
    whole = lax.all_gather(shard, ALL, axis=0, tiled=False)
    whole = whole.reshape(n_dp, n_e, n_h, count, rows, columns)
    return pl.pallas_call(
        unpack_kernel,
        grid=(n_dp * n_h,),
        in_specs=[
            pl.BlockSpec(
                (1, n_e, 1, count, rows, columns), lambda r: (r // n_h, 0, r % n_h, 0, 0, 0)
            )
        ],
        out_specs=[pl.BlockSpec((rows, n * D), lambda r: (r, 0)) for n in units],
        out_shape=[shaped((D, n * D), BF16) for n in units],
        compiler_params=pltpu.CompilerParams(vmem_limit_bytes=32 << 20),
        cost_estimate=pl.CostEstimate(
            flops=0, bytes_accessed=4 * count * D * D, transcendentals=0
        ),
    )(still(whole))


def unpack_steps_kernel(base, *refs):
    pieces, outs = refs[:8], refs[8:]
    own, other = pieces[:4], pieces[4:]
    groups, _, rows, width = own[0].shape

    def fill(k):
        for arrays, core in ((own, base[0]), (other, 1 - base[0])):
            place, at = pl.ds(pl.multiple_of(core * rows, rows), rows), 0
            for out in outs:
                for u in range(out.shape[1] // D):
                    for e in range(groups):
                        column = pl.multiple_of(u * D + (e ^ base[2]) * width, width)
                        out[place, pl.ds(column, width)] = arrays[k][e, at + u]
                at += out.shape[1] // D

    for k in range(4):
        pl.when(pl.program_id(0) == k)(functools.partial(fill, k))


def dense_gather_steps(shard, units, ahead):
    count, rows, columns = shard.shape
    wide = jnp.stack(passed([shard] * 4, EXPERT))
    own = passed([wide] * 4, PLANE)
    own[1], ahead = tie(own[1], ahead)
    other = [swap(piece) for piece in own]
    base = [lax.axis_index(a) for a in (HC, PLANE, EXPERT)]
    whole = pl.BlockSpec(wide.shape, lambda k, at: (0, 0, 0, 0))
    out = pl.pallas_call(
        unpack_steps_kernel,
        grid_spec=pltpu.PrefetchScalarGridSpec(
            num_scalar_prefetch=1,
            grid=(4,),
            in_specs=[whole] * 8,
            out_specs=[pl.BlockSpec((2 * rows, n * D), lambda k, at: (k ^ at[1], 0)) for n in units],
        ),
        out_shape=[shaped((D, n * D), BF16) for n in units],
        compiler_params=pltpu.CompilerParams(vmem_limit_bytes=40 << 20),
        cost_estimate=pl.CostEstimate(
            flops=0, bytes_accessed=4 * count * D * D, transcendentals=0
        ),
    )(jnp.stack(base), *own, *other)
    return out, ahead


def pack_kernel(count, extra, base, *refs):
    grads, added, outs = refs[:count], refs[count : count + extra], refs[count + extra :]
    groups, width = outs[0].shape[-4], outs[0].shape[-1]

    def fill(out, head, other):
        at = 0
        for ref in grads:
            for k in range(ref.shape[1] // width):
                piece = ref[:, k * width : (k + 1) * width]
                e, place = (k % groups) ^ base[2], at + k // groups
                if other is not None:
                    piece = (piece.astype(F32) + other[e, place].astype(F32)).astype(BF16)
                out[head + (e, place)] = piece
            at += ref.shape[1] // (width * groups)

    if len(outs) == 1 and not extra:
        fill(outs[0], (0,), None)
        return
    for p in range(max(len(outs), extra)):
        out, head = (outs[0], (0,)) if len(outs) == 1 else (outs[p], ())
        pl.when(pl.program_id(0) == p)(functools.partial(fill, out, head, added[p] if extra else None))


def dense_pack(grads, core, turned, listed, added=()):
    n_e, n_p, n_c = lax.axis_size(EXPERT), lax.axis_size(PLANE), lax.axis_size(HC)
    count = sum(g.shape[1] for g in grads) // D
    rows, columns = D // (n_p * n_c), D // n_e
    shape = (n_p, n_e, count, rows, columns)
    base = [core] + [lax.axis_index(a) if turned else 0 for a in (PLANE, EXPERT)]
    piece = pl.BlockSpec((1,) + shape[1:], lambda p, at: (p, 0, 0, 0, 0))
    whole = pl.BlockSpec(shape[1:], lambda p, at: (0, 0, 0, 0))
    specs = [
        pl.BlockSpec((rows, g.shape[1]), lambda p, at: ((p ^ at[1]) * n_c + at[0], 0)) for g in grads
    ]
    out = pl.pallas_call(
        functools.partial(pack_kernel, len(grads), len(added)),
        grid_spec=pltpu.PrefetchScalarGridSpec(
            num_scalar_prefetch=1,
            grid=(n_p,),
            in_specs=specs + [whole] * len(added),
            out_specs=[whole] * n_p if listed else piece,
        ),
        out_shape=[shaped(shape[1:], BF16)] * n_p if listed else shaped(shape, BF16),
        compiler_params=pltpu.CompilerParams(vmem_limit_bytes=40 << 20),
        cost_estimate=pl.CostEstimate(
            flops=0, bytes_accessed=4 * count * D * D // n_c, transcendentals=0
        ),
    )(
        jnp.stack([jnp.asarray(b, jnp.int32) for b in base]),
        *[still(v) for v in list(grads) + list(added)],
    )
    return list(out) if listed else out


def dense_other(grads, turned, after=()):
    if lax.axis_size(HC) == 1:
        return [], list(after)
    pieces, after = tie(dense_pack(grads, 1 - lax.axis_index(HC), turned, True), after)
    return [swap(piece) for piece in pieces], after


def dense_both(grads, other, turned):
    core = lax.axis_index(HC) if other else 0
    return dense_pack(grads, core, turned, turned, other)


def dense_expert(pieces):
    parts = summed(pieces).astype(BF16)
    return passed([parts[k] for k in range(parts.shape[0])], EXPERT)


def expert_shard(up, down):
    up, down = up.astype(BF16), down.astype(BF16)
    depth = up.shape[1]
    down = down.reshape(down.shape[0], -1, depth, depth).swapaxes(1, 2).reshape(up.shape)
    both = jnp.stack([up, down], axis=1)
    if lax.axis_size(HC) == 1:
        return both[0]
    me = lax.axis_index(HC)
    return jnp.concatenate([take(both, 0, me), swap(take(both, 0, 1 - me))], axis=2)


def gather_rows(in_ref, out, parts):
    _, capacity, width = in_ref.shape
    for i in range(in_ref.shape[0]):
        g, p = i // parts, i % parts
        out[g * capacity : (g + 1) * capacity, p * width : (p + 1) * width] = in_ref[i]


def part_rows(value, out_ref, parts):
    _, capacity, width = out_ref.shape
    for i in range(out_ref.shape[0]):
        g, p = i // parts, i % parts
        rows = value[g * capacity : (g + 1) * capacity, p * width : (p + 1) * width]
        out_ref[i] = rows.astype(out_ref.dtype)


def expert_kernel(parts, n_dp, base, x_ref, *refs):
    weights, (y_ref, x, y) = refs[:-3], refs[-3:]
    _, _, depth, width = weights[0].shape
    step, each = pl.program_id(0), len(weights) // n_dp

    @pl.when(step == 0)
    def _():
        gather_rows(x_ref, x, parts)
        y[...] = jnp.zeros_like(y)

    cuts = [slice(i * depth, (i + 1) * depth) for i in range(n_dp)]
    blocks = [slice(i, i + depth) for i in range(0, width, depth)]
    for n in range(each):
        own = [weights[i * each + n] for i in range(n_dp)]
        u = sum(contract(x[:, cuts[i]], own[i][0, 0], 1, 0) for i in range(n_dp))
        hidden = (u * jax.nn.sigmoid(u)).astype(BF16)
        for i in range(n_dp):
            y[:, cuts[i]] += sum(contract(hidden[:, b], own[i][0, 1, :, b], 1, 0) for b in blocks)

    @pl.when(step == pl.num_programs(0) - 1)
    def _():
        part_rows(y[...], y_ref, parts)


def expert_back_kernel(parts, n_dp, base, x_ref, g_ref, *refs):
    weights, (dx_ref, dw_ref, x, g, dx) = refs[:-5], refs[-5:]
    _, _, depth, width = weights[0].shape
    step, each = pl.program_id(0), len(weights) // n_dp

    @pl.when(step == 0)
    def _():
        gather_rows(x_ref, x, parts)
        gather_rows(g_ref, g, parts)
        dx[...] = jnp.zeros_like(dx)

    cuts = [slice(i * depth, (i + 1) * depth) for i in range(n_dp)]
    blocks = [slice(i, i + depth) for i in range(0, width, depth)]
    for n in range(each):
        own = [weights[i * each + n] for i in range(n_dp)]
        u = sum(contract(x[:, cuts[i]], own[i][0, 0], 1, 0) for i in range(n_dp))
        logistic = jax.nn.sigmoid(u)
        hidden = (u * logistic).astype(BF16)
        dh = [sum(contract(g[:, cuts[i]], own[i][0, 1, :, b], 1, 1) for i in range(n_dp)) for b in blocks]
        dh = jnp.concatenate(dh, axis=1)
        du = (dh * (logistic * (1.0 + u * (1.0 - logistic)))).astype(BF16)
        for i in range(n_dp):
            at = (i * each + n) ^ base[0]
            dw_ref[at, 0] = contract(x[:, cuts[i]], du, 0, 0).astype(BF16)
            for b in blocks:
                dw_ref[at, 1, :, b] = contract(hidden[:, b], g[:, cuts[i]], 0, 0).astype(BF16)
            dx[:, cuts[i]] += contract(du, own[i][0, 0], 1, 1)

    @pl.when(step == pl.num_programs(0) - 1)
    def _():
        part_rows(dx[...], dx_ref, parts)


def expert_call(pieces, weights, grads=None):
    parts = D // pieces.shape[2]
    n_dp, count = lax.axis_size(DP), lax.axis_size(PLANE)
    turned = isinstance(weights, list)
    arrays = [w[None] for w in weights] if turned else [weights] * count
    _, _, depth, width = arrays[0].shape
    cut = min(width, 512)
    rows = pieces.size // D
    base = jnp.reshape(lax.axis_index(PLANE) if turned else jnp.int32(0), (1,)).astype(jnp.int32)
    whole = pl.BlockSpec(pieces.shape, lambda c, at: (0, 0, 0))
    slabs = [
        pl.BlockSpec((1, 2, depth, cut), lambda c, at, k=0 if turned else k: (k, 0, 0, c))
        for k in range(count)
    ]
    shape = jax.ShapeDtypeStruct(pieces.shape, BF16)
    kept = pltpu.VMEM((rows, D), BF16)
    if grads is None:
        return pl.pallas_call(
            functools.partial(expert_kernel, parts, n_dp),
            grid_spec=pltpu.PrefetchScalarGridSpec(
                num_scalar_prefetch=1,
                grid=(width // cut,),
                in_specs=[whole] + slabs,
                out_specs=whole,
                scratch_shapes=[kept, pltpu.VMEM((rows, D), F32)],
            ),
            out_shape=shape,
            compiler_params=pltpu.CompilerParams(vmem_limit_bytes=40 << 20),
            cost_estimate=pl.CostEstimate(
                flops=4 * rows * D * EFF, bytes_accessed=4 * D * EFF, transcendentals=rows * EFF
            ),
        )(base, pieces, *[still(a) for a in arrays])
    return pl.pallas_call(
        functools.partial(expert_back_kernel, parts, n_dp),
        grid_spec=pltpu.PrefetchScalarGridSpec(
            num_scalar_prefetch=1,
            grid=(width // cut,),
            in_specs=[whole, whole] + slabs,
            out_specs=[whole, pl.BlockSpec((count, 2, depth, cut), lambda c, at: (0, 0, 0, c))],
            scratch_shapes=[kept, kept, pltpu.VMEM((rows, D), F32)],
        ),
        out_shape=[shape, shaped((count, 2, depth, width), BF16)],
        compiler_params=pltpu.CompilerParams(vmem_limit_bytes=40 << 20),
        cost_estimate=pl.CostEstimate(
            flops=12 * rows * D * EFF, bytes_accessed=8 * D * EFF, transcendentals=rows * EFF
        ),
    )(base, pieces, grads, *[still(a) for a in arrays])


def rotate(value, cosine, sine):
    low, high = value[..., :HALF, :], value[..., HALF:, :]
    return jnp.concatenate([low * cosine - high * sine, low * sine + high * cosine], axis=-2)


def unrotate(value, cosine, sine):
    low, high = value[..., :HALF, :], value[..., HALF:, :]
    return jnp.concatenate([low * cosine + high * sine, high * cosine - low * sine], axis=-2)


def contract(left, right, left_dim, right_dim):
    return lax.dot_general(
        left, right, (((left_dim,), (right_dim,)), ((), ())), preferred_element_type=F32
    )


def masked_scores(raw, low, high, base):
    place = base + lax.broadcasted_iota(jnp.int32, raw.shape, 0)
    return jnp.where((place >= low) & (place < high), raw, NEG)


def attend_kernel(unroll, span_ref, q_ref, k_ref, v_ref, o_ref, full_ref, lse_ref, scratch):
    count, width = k_ref.shape[0], k_ref.shape[-1]

    def one(j, _):
        low, high = span_ref[j, 0:1], span_ref[j, 1:2]
        query, scores = q_ref[j, 0, 0], scratch.at[j % unroll]
        peak = None
        for i in range(count):
            part = masked_scores(contract(k_ref[i, 0, 0], query, 0, 0), low, high, i * width)
            scores[i] = part
            top = jnp.max(part, axis=0, keepdims=True)
            peak = top if peak is None else jnp.maximum(peak, top)
        total = jnp.zeros_like(peak)
        mixed = jnp.zeros(query.shape, F32)
        for i in range(count):
            part = jnp.exp(scores[i] - peak)
            total = total + jnp.sum(part, axis=0, keepdims=True)
            mixed = mixed + contract(v_ref[i, 0, 0], part.astype(BF16), 1, 0)
        mixed = mixed * (1.0 / total)
        o_ref[j, 0] = mixed.astype(BF16)
        full_ref[j, 0] = mixed
        lse_ref[j, 0] = peak + jnp.log(total)
        return 0

    lax.fori_loop(0, q_ref.shape[0], one, 0, unroll=unroll)


def attend_back_kernel(
    unroll, together, span_ref, rot_q, rot_k, q_ref, k_ref, v_ref, g_ref, full_ref, lse_ref, *refs
):
    dk, dv, kt, vt = refs[-4:]
    dkv_ref, base = refs[-5], 1 if together else 0
    count, width = k_ref.shape[0], k_ref.shape[-1]
    dk[...] = jnp.zeros_like(dk)
    dv[...] = jnp.zeros_like(dv)
    for i in range(count):
        kt[i] = k_ref[i, 0, 0].T
        vt[i] = v_ref[i, 0, 0].T

    def one(j, _):
        low, high = span_ref[j, 0:1], span_ref[j, 1:2]
        query, grad, log_total = q_ref[j, 0, 0], g_ref[j, 0], lse_ref[j, 0]
        query_turned, grad_turned = query.T, grad.T
        delta = jnp.sum(grad.astype(F32) * full_ref[j, 0], axis=0, keepdims=True)

        def slopes(i):
            raw = masked_scores(contract(kt[i], query, 1, 0), low, high, i * width)
            part = jnp.exp(raw - log_total)
            slope = part * (contract(vt[i], grad, 1, 0) - delta)
            return part.astype(BF16), slope.astype(BF16)

        dq = jnp.zeros(query.shape, F32)
        coming = slopes(0)
        for i in range(count):
            part, slope = coming
            if i + 1 < count:
                coming = slopes(i + 1)
            dv[i] += contract(part, grad_turned, 1, 0)
            dk[i] += contract(slope, query_turned, 1, 0)
            dq = dq + contract(k_ref[i, 0, 0], slope, 1, 0)
        dq = unrotate(dq * HD ** (-0.5), rot_q[j, 0], rot_q[j, 1]).astype(BF16)
        if together:
            dkv_ref[j, 0, 0] = dq
        else:
            refs[0][j, 0] = dq
        return 0

    lax.fori_loop(0, q_ref.shape[0], one, 0, unroll=unroll)
    for i in range(count):
        dkv_ref[i, base, 0] = unrotate(dk[i].T, rot_k[i, 0], rot_k[i, 1]).astype(BF16)
        dkv_ref[i, base + 1, 0] = dv[i].T.astype(BF16)


def head_spec(block, part=None):
    if part is None:
        shape = (block.shape[0], 1) + block.shape[2:]
        return pl.BlockSpec(shape, lambda h: (0, h, 0, 0))
    shape = (block.shape[0], 1, 1) + block.shape[3:]
    return pl.BlockSpec(shape, lambda h: (0, part, h, 0, 0))


def attend(spans, queries, keys, first):
    nq, _, heads, _, width = queries.shape
    nk, unroll = keys.shape[0], min(4, nq)
    outs = [
        jax.ShapeDtypeStruct((nq, heads, HD, width), BF16),
        jax.ShapeDtypeStruct((nq, heads, HD, width), F32),
        jax.ShapeDtypeStruct((nq, heads, 1, width), F32),
    ]
    return pl.pallas_call(
        functools.partial(attend_kernel, unroll),
        grid=(heads,),
        in_specs=[
            pl.BlockSpec(spans.shape, lambda h: (0, 0, 0)),
            head_spec(queries, 0),
            head_spec(keys, first),
            head_spec(keys, first + 1),
        ],
        out_specs=[head_spec(o) for o in outs],
        out_shape=outs,
        scratch_shapes=[pltpu.VMEM((unroll, nk, width, width), F32)],
        compiler_params=pltpu.CompilerParams(vmem_limit_bytes=40 << 20),
        cost_estimate=pl.CostEstimate(
            flops=4 * heads * nq * nk * width * width * HD,
            bytes_accessed=4 * heads * (nq + nk) * HD * width,
            transcendentals=heads * nq * nk * width * width,
        ),
    )(spans, queries, keys, keys)


def attend_back(spans, rot_q, rot_k, queries, keys, first, grads, full, log_total):
    nq, _, heads, _, width = queries.shape
    nk = keys.shape[0]
    together = nq == nk
    outs = [jax.ShapeDtypeStruct((nk, 3 if together else 2, heads, HD, width), BF16)]
    out_specs = [pl.BlockSpec(outs[0].shape[:2] + (1, HD, width), lambda h: (0, 0, h, 0, 0))]
    if not together:
        outs.insert(0, jax.ShapeDtypeStruct((nq, heads, HD, width), BF16))
        out_specs.insert(0, head_spec(outs[0]))
    whole = lambda v: pl.BlockSpec(v.shape, lambda h: (0,) * len(v.shape))
    return pl.pallas_call(
        functools.partial(attend_back_kernel, min(2, nq), together),
        grid=(heads,),
        in_specs=[
            whole(spans),
            whole(rot_q),
            whole(rot_k),
            head_spec(queries, 0),
            head_spec(keys, first),
            head_spec(keys, first + 1),
            head_spec(grads),
            head_spec(full),
            head_spec(log_total),
        ],
        out_specs=out_specs,
        out_shape=outs,
        scratch_shapes=[pltpu.VMEM((nk, width, HD), F32)] * 2 + [pltpu.VMEM((nk, width, HD), BF16)] * 2,
        compiler_params=pltpu.CompilerParams(vmem_limit_bytes=40 << 20),
        cost_estimate=pl.CostEstimate(
            flops=10 * heads * nq * nk * width * width * HD,
            bytes_accessed=8 * heads * (nq + nk) * HD * width,
            transcendentals=heads * nq * nk * width * width,
        ),
    )(spans, rot_q, rot_k, queries, keys, keys, grads, full, log_total)


def build_tables(lengths, routes, rows):
    axes = frame_axes()
    total = rows * lax.axis_size(axes)
    order = lax.axis_index(axes)
    lengths = take(lengths, 0, lax.axis_index(EB))
    ends = jnp.cumsum(lengths)
    starts = ends - lengths
    places = jnp.arange(total, dtype=jnp.int32)
    segment = jnp.sum((places[:, None] >= ends[None, :]).astype(jnp.int32), axis=-1)
    member = segment[:, None] == jnp.arange(lengths.shape[0], dtype=jnp.int32)
    low = jnp.sum(jnp.where(member, starts, 0), axis=-1)
    high = jnp.sum(jnp.where(member, ends, 0), axis=-1)
    spans = jnp.stack([low, high]).reshape(2, -1, rows).swapaxes(0, 1)
    position = (places - low).reshape(-1, 1, rows)
    frequency = 10000.0 ** (-jnp.arange(HALF, dtype=F32) * 2.0 / HD)
    angles = position.astype(F32) * frequency[:, None]
    rotary = jnp.stack([jnp.cos(angles), jnp.sin(angles)], axis=1)
    wide = jnp.pad(segment, (RIM, RIM), constant_values=-1)
    wide = lax.dynamic_slice_in_dim(wide, order * rows, rows + 2 * RIM)
    own = wide[RIM : RIM + rows]
    masks = jnp.stack([(wide[i : i + rows] == own).astype(F32) for i in range(KER)], axis=1)

    routes = routes[..., 0]
    if paired():
        mine = lax.axis_index(HC) == lax.axis_index(ES)
        other = swap(routes)
        routes = jnp.where(mine, routes, other)
    chosen = take(routes, 0, lax.axis_index(EB))
    block = chosen.shape[0]
    capacity = 3 * block // 16
    experts = jnp.arange(EXPERTS, dtype=jnp.int32)
    onehot = chosen[:, None] == experts
    earlier = jnp.tril(jnp.ones((block, block), BF16), -1)
    slots = jnp.sum(jnp.where(onehot, dot(earlier, onehot.astype(BF16), 1, 0), 0.0), axis=-1)
    slots = slots.astype(jnp.int32)
    parts = lax.axis_size(sub_axis())
    sub = lax.axis_index(sub_axis())
    own_chosen = take(chosen.reshape(parts, -1), 0, sub)
    if paired():
        flip = lambda v: jnp.where(sub == 0, v, jnp.roll(v, block // 2))
        chosen, slots = flip(chosen), flip(slots)
    place = chosen * capacity + slots
    table = (jnp.arange(EXPERTS * capacity, dtype=jnp.int32)[:, None] == place).astype(BF16)
    if paired():
        table = (table[:, : block // 2], table[:, block // 2 :])
    own_onehot = (own_chosen[:, None] == experts).astype(F32)
    return spans, rotary, take(rotary, 0, order), take(spans, 0, order), masks, table, own_onehot


def rims(block):
    axes = (ES, HX, HC)
    sizes = [lax.axis_size(axis) for axis in axes]
    order = np.arange(math.prod(sizes)).reshape(sizes)
    order = [int(i) for i in np.transpose(order, [axes.index(a) for a in frame_axes()]).flat]
    low = lax.ppermute(block[-EDGE:], axes, list(zip(order[:-1], order[1:])))
    high = lax.ppermute(block[:EDGE], axes, list(zip(order[1:], order[:-1])))
    return low, high


def to_experts(halves, table):
    if paired():
        own, other = halves[0], swap(halves[1])
        sent = (dot(table[0], own, 1, 0) + dot(table[1], other, 1, 0)).astype(BF16)
    else:
        wide = lax.all_to_all(halves[0], ES, split_axis=1, concat_axis=0, tiled=True)
        sent = dot(table, wide, 1, 0).astype(BF16)
    return exchange(sent.reshape(EXPERTS, -1, sent.shape[1]), MOE)


def from_experts(pieces, table):
    got = exchange(pieces, MOE).reshape(EXPERTS * pieces.shape[1], -1)
    if paired():
        other = swap(dot(table[1], got, 0, 0).astype(BF16))
        return dot(table[0], got, 0, 0).astype(BF16), other
    return (lax.all_to_all(dot(table, got, 0, 0).astype(BF16), ES, split_axis=0, concat_axis=1, tiled=True),)


def heads_apart(block):
    if lax.axis_size(frame_axes()) == HEADS:
        got = exchange(block, frame_axes())[:, :, None]
        return got, got, 1
    block = jnp.swapaxes(block, 0, 1)
    return block[None, :1], lax.all_gather(block[1:], frame_axes(), axis=0, tiled=False), 0


def heads_together(block):
    if lax.axis_size(frame_axes()) == HEADS:
        block = exchange(block, frame_axes())
    return block.reshape(HEADS * HD, -1)


def heads_grad(block):
    if lax.axis_size(frame_axes()) == HEADS:
        return exchange(block, frame_axes())[:, None]
    return block[None]


def heads_back(grads):
    if len(grads) == 1:
        return exchange(grads[0][:, :, 0], frame_axes())
    dq, dkv = grads
    dkv = lax.psum_scatter(dkv, frame_axes(), scatter_dimension=0, tiled=False)
    return jnp.swapaxes(jnp.concatenate([dq, dkv], axis=0), 0, 1)


def unit(value):
    return lax.rsqrt(jnp.mean(value * value, axis=-1, keepdims=True) + EPS)


def normed(value, gain):
    return (value * unit(value) * gain).astype(BF16)


def norm_back(upstream, value, gain):
    factor = unit(value)
    gain_grad = jnp.sum(upstream * value * factor, axis=0, keepdims=True)
    scaled = gain * upstream
    mixed = jnp.sum(scaled * value, axis=-1, keepdims=True)
    return factor * scaled - value * (factor**3 * mixed / D), gain_grad


def joined(part, halves):
    if len(halves) == 1:
        return halves[0][...].astype(F32)
    own, other = halves[0][...].astype(F32), halves[1][...].astype(F32)
    first = part == 0
    return jnp.concatenate([jnp.where(first, own, other), jnp.where(first, other, own)], axis=1)


def give_halves(part, value, refs):
    if len(refs) == 1:
        refs[0][...] = value
        return
    low, high = value[:, : D // 2], value[:, D // 2 :]
    first = part == 0
    refs[0][...] = jnp.where(first, low.astype(F32), high.astype(F32)).astype(BF16)
    refs[1][...] = jnp.where(first, high.astype(F32), low.astype(F32)).astype(BF16)


def half_shapes(rows):
    count = 2 if paired() else 1
    return [jax.ShapeDtypeStruct((rows, D // count), BF16)] * count


def fused(kernel, scalar, args, out_shape, flops, grid=(), in_specs=None, out_specs=None, scratch=()):
    whole = lambda v: pl.BlockSpec(v.shape, lambda *at, n=len(v.shape): (0,) * n)
    in_specs = [spec or whole(a) for spec, a in zip(in_specs or [None] * len(args), args)]
    out_specs = [spec or whole(o) for spec, o in zip(out_specs or [None] * len(out_shape), out_shape)]
    size = sum(math.prod(v.shape) * v.dtype.itemsize for v in list(args) + list(out_shape))
    return pl.pallas_call(
        kernel,
        grid_spec=pltpu.PrefetchScalarGridSpec(
            num_scalar_prefetch=1,
            grid=grid or (1,),
            in_specs=in_specs,
            out_specs=out_specs,
            scratch_shapes=list(scratch),
        ),
        out_shape=out_shape,
        compiler_params=pltpu.CompilerParams(vmem_limit_bytes=56 << 20),
        cost_estimate=pl.CostEstimate(flops=flops, bytes_accessed=size, transcendentals=0),
    )(jnp.reshape(jnp.asarray(0 if scalar is None else scalar, jnp.int32), (1,)), *[still(a) for a in args])


def enter_kernel(halves, part, *refs):
    if halves:
        x3, gate, below = refs[:3]
        backs, refs = refs[3 : 3 + halves], refs[3 + halves :]
        gains, wi, wo, qkv, rot, x_ref, x1_ref, t_ref, a0, y = refs
    else:
        x_ref, gains, wi, wo, qkv, rot, x1_ref, t_ref, a0, y = refs
    step = pl.program_id(0)

    @pl.when(step == 0)
    def _():
        if halves:
            x4 = x3[...] + 0.5 * gate[...] * joined(part[0], backs)
            x_ref[...] = x4 * unit(x4) * below[4:5]
        a0[...] = normed(x_ref[...], gains[0:1])
        y[...] = jnp.zeros_like(y)

    u = contract(a0[...], wi[...], 1, 0)
    y[...] += contract((u * jax.nn.sigmoid(u)).astype(BF16), wo[...], 1, 1)

    @pl.when(step == pl.num_programs(0) - 1)
    def _():
        x1 = x_ref[...] + 0.5 * y[...]
        x1_ref[...] = x1
        t = contract(normed(x1, gains[1:2]), qkv[...], 1, 0).T
        cosine, sine = rot[0], rot[1]
        for h in range(HEADS):
            own = [t[w * D + h * HD : w * D + (h + 1) * HD] for w in range(3)]
            t_ref[h, 0] = (rotate(own[0], cosine, sine) * HD ** (-0.5)).astype(BF16)
            t_ref[h, 1] = rotate(own[1], cosine, sine).astype(BF16)
            t_ref[h, 2] = own[2].astype(BF16)


def enter(part, x, below, gains, ffn_in, ffn_out, qkv, rot):
    rows = (x if below is None else below[0]).shape[0]
    steps = ffn_in.shape[1] // D
    column = pl.BlockSpec((D, D), lambda j, at: (0, j))
    stream = jax.ShapeDtypeStruct((rows, D), F32)
    heads = jax.ShapeDtypeStruct((HEADS, 3, HD, rows), BF16)
    own = [gains, ffn_in, ffn_out, qkv, rot]
    if below is None:
        lead, outs = [x], [stream, heads]
    else:
        x3, gate, halves, above = below
        lead, outs = [x3, gate, above] + list(halves), [stream, stream, heads]
    out = fused(
        functools.partial(enter_kernel, 0 if below is None else len(below[2])),
        part,
        lead + own,
        outs,
        2 * rows * D * (2 * ffn_in.shape[1] + 3 * D),
        grid=(steps,),
        in_specs=[None] * len(lead) + [None, column, column, None, None],
        scratch=[pltpu.VMEM((rows, D), BF16), pltpu.VMEM((rows, D), F32)],
    )
    return (x,) + tuple(out) if below is None else tuple(out)


def middle_kernel(part, x1, o, attn_out, glu, gains, x2_ref, z_ref):
    x2 = x1[...] + contract(o[...], attn_out[...], 0, 1)
    x2_ref[...] = x2
    g = contract(normed(x2, gains[2:3]), glu[...], 1, 0)
    z_ref[...] = (g[:, :D] * jax.nn.sigmoid(g[:, D:])).astype(BF16)


def fill_wide(wide, low, block, high):
    rows = block.shape[0]
    wide[0:EDGE] = low[...].astype(F32)
    wide[EDGE : EDGE + rows] = block[...].astype(F32)
    wide[EDGE + rows :] = high[...].astype(F32)


def fill_masks(valid, masks):
    for i in range(KER):
        valid[i] = jnp.broadcast_to(masks[:, i : i + 1], valid.shape[1:])


def tiles(rows):
    size = min(rows, 64)
    return [(r, c, size) for c in range(0, D, 128) for r in range(0, rows, size)]


def conv_kernel_body(
    halves, part, x2, z, low, high, masks, taps, conv_out, gains, router, onehot, *refs
):
    x3_ref, c_ref, gate_ref = refs[:3]
    gives, wide, valid = refs[3 : 3 + halves], refs[-2], refs[-1]
    fill_wide(wide, low, z, high)
    fill_masks(valid, masks)
    for r, c, size in tiles(z.shape[0]):
        total = jnp.zeros((size, 128), F32)
        for i in range(KER):
            first = r + i + EDGE - RIM
            term = wide[first : first + size, c : c + 128] * valid[i, r : r + size]
            total = total + taps[i : i + 1, c : c + 128] * term
        c_ref[r : r + size, c : c + 128] = total
    mixed = c_ref[...]
    e = (mixed * jax.nn.sigmoid(mixed)).astype(BF16)
    x3 = x2[...] + contract(e, conv_out[...], 1, 1)
    x3_ref[...] = x3
    a3 = normed(x3, gains[3:4])
    gate_ref[...] = jnp.sum(softmax(contract(a3, router[...], 1, 1)) * onehot[...], axis=-1, keepdims=True)
    give_halves(part[0], a3, gives)


def softmax(logits):
    grown = jnp.exp(logits - jnp.max(logits, axis=-1, keepdims=True))
    return grown / jnp.sum(grown, axis=-1, keepdims=True)


def turn(upstream, x3, gate, back, gain):
    x4 = x3 + 0.5 * gate * back
    dx4, gain_grad = norm_back(upstream, x4, gain)
    half = 0.5 * dx4
    dgate = jnp.sum(half * back, axis=-1, keepdims=True)
    return x4, dx4, dgate, (gate * half).astype(BF16), gain_grad


def turn_kernel(halves, part, upstream, x3, gate, gains, *refs):
    backs, (out_ref, dx4_ref, dgate_ref, small_ref), gives = refs[:halves], refs[halves : halves + 4], refs[halves + 4 :]
    x4, dx4, dgate, sent, gain_grad = turn(
        upstream[...].astype(F32), x3[...], gate[...], joined(part[0], backs), gains[4:5]
    )
    out_ref[...] = (x4 * unit(x4) * gains[4:5]).astype(BF16)
    dx4_ref[...] = dx4
    dgate_ref[...] = dgate
    small_ref[...] = jnp.broadcast_to(gain_grad, small_ref.shape)
    give_halves(part[0], sent, gives)


def experts_back_kernel(
    halves, part, dx4, dgate, x3, mixed, gains, router, onehot, conv_out, *refs
):
    backs, (dx3_ref, dc_ref, dy2_ref, e_ref, small_ref) = refs[:halves], refs[halves:]
    a3 = normed(x3[...], gains[3:4])
    probs = softmax(contract(a3, router[...], 1, 1))
    gate = jnp.sum(probs * onehot[...], axis=-1, keepdims=True)
    dlogits = dgate[...] * probs * (onehot[...] - gate)
    wide = lambda a, b, i, j: lax.dot_general(
        a, b, (((i,), (j,)), ((), ())), preferred_element_type=F32, precision=BEST
    )
    da3 = joined(part[0], backs) + wide(dlogits, router[...].astype(F32), 1, 0)
    dn, gain_grad = norm_back(da3, x3[...], gains[3:4])
    dx3 = dx4[...] + dn
    dx3_ref[...] = dx3
    dy2 = dx3.astype(BF16)
    c = mixed[...]
    logistic = jax.nn.sigmoid(c)
    dy2_ref[...] = dy2
    e_ref[...] = (c * logistic).astype(BF16)
    slope = logistic * (1.0 + c * (1.0 - logistic))
    dc_ref[...] = (contract(dy2, conv_out[...], 1, 0) * slope).astype(BF16)
    small_ref[0:EXPERTS] = wide(dlogits, a3.astype(F32), 0, 0)
    small_ref[EXPERTS : 2 * EXPERTS] = jnp.broadcast_to(gain_grad, (EXPERTS, D))


def conv_back_kernel(
    part, dc, dlow, dhigh, z, low, high, masks, taps, x2, dx3, glu, attn_out, gains,
    dx2_ref, do_ref, a2_ref, dg_ref, dy1_ref, small_ref, wide, dwide, valid, dz,
):
    fill_wide(wide, low, z, high)
    fill_wide(dwide, dlow, dc, dhigh)
    fill_masks(valid, masks)
    small_ref[...] = jnp.zeros_like(small_ref)
    for r, c, size in tiles(z.shape[0]):
        own = dwide[EDGE + r : EDGE + r + size, c : c + 128]
        total = jnp.zeros((size, 128), F32)
        for i in range(KER):
            first = r + i + EDGE - RIM
            value = valid[i, r : r + size]
            term = own * (wide[first : first + size, c : c + 128] * value)
            small_ref[i : i + 1, c : c + 128] += jnp.sum(term, axis=0, keepdims=True)
            tap = taps[KER - 1 - i : KER - i, c : c + 128]
            total = total + tap * (dwide[first : first + size, c : c + 128] * value)
        dz[r : r + size, c : c + 128] = total
    a2 = normed(x2[...], gains[2:3])
    g = contract(a2, glu[...], 1, 0)
    g0, logistic = g[:, :D], jax.nn.sigmoid(g[:, D:])
    grad = dz[...]
    dg = [(grad * logistic).astype(BF16), (grad * g0 * logistic * (1.0 - logistic)).astype(BF16)]
    dn = contract(dg[0], glu[:, :D], 1, 1) + contract(dg[1], glu[:, D:], 1, 1)
    dn, gain_grad = norm_back(dn, x2[...], gains[2:3])
    small_ref[KER : KER + 1] = gain_grad
    dx2 = dx3[...] + dn
    dx2_ref[...] = dx2
    dy1 = dx2.astype(BF16)
    turned = contract(dy1, attn_out[...], 1, 0).T
    do_ref[...] = turned.astype(BF16).reshape(do_ref.shape)
    a2_ref[...] = a2
    dy1_ref[...] = dy1
    for k in range(2):
        dg_ref[:, k * D : (k + 1) * D] = dg[k]


def enter_back_kernel(
    halves, part, dt, x1, x, dx2, qkv, wi, wo, gains, *refs
):
    if halves:
        x3, gate, below = refs[:3]
        backs, refs = refs[3 : 3 + halves], refs[3 + halves :]
        dx_ref, dgate_ref = refs[:2]
        gives, refs = refs[2 : 2 + halves], refs[2 + halves :]
    else:
        dx_ref, refs = refs[0], refs[1:]
    turned, a1, a0, dy0, h0, du0, small_ref, dx1, dn0 = refs
    step = pl.program_id(0)

    @pl.when(step == 0)
    def _():
        for h in range(HEADS):
            for w in range(3):
                turned[w * D + h * HD : w * D + (h + 1) * HD] = dt[h, w]
        a1[...] = normed(x1[...], gains[1:2])
        dn, gain_grad = norm_back(contract(turned[...], qkv[...], 0, 1), x1[...], gains[1:2])
        small_ref[...] = jnp.zeros_like(small_ref)
        small_ref[1:2] = gain_grad
        grad = dx2[...] + dn
        dx1[...] = grad
        dy0[...] = (0.5 * grad).astype(BF16)
        a0[...] = normed(x[...], gains[0:1])
        dn0[...] = jnp.zeros_like(dn0)

    u = contract(a0[...], wi[...], 1, 0)
    logistic = jax.nn.sigmoid(u)
    h0[...] = (u * logistic).astype(BF16)
    slope = logistic * (1.0 + u * (1.0 - logistic))
    du = (contract(dy0[...], wo[...], 1, 0) * slope).astype(BF16)
    du0[...] = du
    dn0[...] += contract(du, wi[...], 1, 1)

    @pl.when(step == pl.num_programs(0) - 1)
    def _():
        dn, gain_grad = norm_back(dn0[...], x[...], gains[0:1])
        small_ref[0:1] = gain_grad
        dx = dx1[...] + dn
        if halves:
            _, dx4, dgate, sent, gain_grad = turn(
                dx, x3[...], gate[...], joined(part[0], backs), below[4:5]
            )
            dx_ref[...] = dx4
            dgate_ref[...] = dgate
            small_ref[4:5] = gain_grad
            give_halves(part[0], sent, gives)
        else:
            dx_ref[...] = dx.astype(BF16)


def enter_back(part, dt, x1, x, dx2, qkv, ffn_in, ffn_out, gains, below):
    rows = x.shape[0]
    column = pl.BlockSpec((D, D), lambda j, at: (0, j))
    args = [dt, x1, x, dx2, qkv, ffn_in, ffn_out, gains]
    in_specs = [None] * 5 + [column, column, None]
    stream = jax.ShapeDtypeStruct((rows, D), F32)
    if below is None:
        lead = [jax.ShapeDtypeStruct((rows, D), BF16)]
    else:
        x3, gate, halves, above = below
        args += [x3, gate, above] + list(halves)
        in_specs += [None] * (3 + len(halves))
        lead = [stream, jax.ShapeDtypeStruct((rows, 1), F32)] + half_shapes(rows)
    low = jax.ShapeDtypeStruct((rows, D), BF16)
    wide = shaped((rows, ffn_in.shape[1]), BF16)
    piece = pl.BlockSpec((rows, D), lambda j, at: (0, j))
    out = fused(
        functools.partial(enter_back_kernel, 0 if below is None else len(below[2])),
        part,
        args,
        lead
        + [shaped((3 * D, rows), BF16), low, low, low, wide, wide, jax.ShapeDtypeStruct((8, D), F32)],
        2 * rows * D * (3 * ffn_in.shape[1] + 3 * D),
        grid=(ffn_in.shape[1] // D,),
        in_specs=in_specs,
        out_specs=[None] * (len(lead) + 4) + [piece, piece, None],
        scratch=[
            pltpu.VMEM((rows, D), F32),
            pltpu.VMEM((rows, D), F32),
        ],
    )
    turned, a1, a0, dy0, h0, du0, small = out[len(lead) :]
    dqkv = dot(a1, turned, 0, 1).astype(BF16)
    dffn_in, dffn_out = dot(a0, du0, 0, 0).astype(BF16), dot(dy0, h0, 0, 0).astype(BF16)
    return out[: len(lead)], (dqkv, dffn_in, dffn_out, small)


def forward_layer(l, x, below, weights, tables, queue, coming):
    ffn_in, qkv, glu, ffn_out, attn_out, conv_out, expert, gains, taps, router = weights
    spans, rotary, own_rotary, own_spans, masks, table, onehot = tables
    rows = own_rotary.shape[-1]
    stream, low = jax.ShapeDtypeStruct((rows, D), F32), jax.ShapeDtypeStruct((rows, D), BF16)
    one = jax.ShapeDtypeStruct((rows, 1), F32)
    x, x1, heads = enter(below and below[4], x, below and below[:4], gains, ffn_in, ffn_out, qkv, own_rotary)
    heads, coming = tie(queue.point((l, -1), heads), coming)
    coming = [dense_gather(shard, UNITS) for shard in coming]
    dense = [None]
    if coming:
        queue.at((l, 8), coming[0], lambda arrays: dense.insert(0, arrays))
    queries, keys, first = heads_apart(heads)
    query_spans = spans if queries.shape[0] > 1 else own_spans[None]
    context, full, log_total = attend(query_spans, queries, keys, first)
    o = heads_together(queue.point((l, 0), context))
    x2, z = fused(
        middle_kernel, 0, [x1, o, attn_out, glu, gains], [stream, low], 6 * rows * D * D
    )
    z_low, z_high = rims(z)
    part = feature_part(isinstance(expert, list))
    x3, c, gate, *halves = fused(
        functools.partial(conv_kernel_body, len(half_shapes(rows))),
        part,
        [x2, z, z_low, z_high, masks, taps, conv_out, gains, router, onehot],
        [stream, stream, one] + half_shapes(rows),
        2 * rows * D * (D + 2 * KER),
        scratch=[pltpu.VMEM((rows + 2 * EDGE, D), F32), pltpu.VMEM((KER, rows, 128), F32)],
    )
    x3 = queue.point((l, 1), x3)
    sent = to_experts(halves, table)
    backs = from_experts(queue.point((l, 8), expert_call(sent, expert)), table)
    saved = (x, x1, queries, keys, full, log_total, o, x2, z, z_low, z_high, c, sent)
    return saved, (x3, gate, backs, gains, part), dense[0]


def backward_layer(l, grads, weights, saved, left, below, tables, queue):
    ffn_in, qkv, glu, ffn_out, attn_out, conv_out, expert, gains, taps, router = weights
    spans, rotary, own_rotary, own_spans, masks, table, onehot = tables
    x, x1, queries, keys, full, log_total, o, x2, z, z_low, z_high, c, sent = saved
    dx4, dgate, halves = grads
    x3, part = left[0], left[4]
    rows = x.shape[0]
    stream, low = jax.ShapeDtypeStruct((rows, D), F32), jax.ShapeDtypeStruct((rows, D), BF16)
    dy = queue.point((l, 2), to_experts(halves, table))
    dsent, dexpert = expert_call(sent, expert, dy)
    total = lax.psum_scatter(dexpert, PLANE, scatter_dimension=0, tiled=False)
    expert_sums = [total]
    if l == 0:
        queue.at((l, 7), [total], lambda arrays: expert_sums.insert(0, arrays[0]))
    dsent = queue.point((l, 3), dsent)
    backs = from_experts(dsent, table)
    dx3, dc, dy2, e, small_one = fused(
        functools.partial(experts_back_kernel, len(backs)),
        part,
        [dx4, dgate, x3, c, gains, router, onehot, conv_out] + list(backs),
        [stream, low, low, low, jax.ShapeDtypeStruct((2 * EXPERTS, D), F32)],
        2 * rows * D * D,
    )
    dconv_out = dot(dy2, e, 0, 0).astype(BF16)
    dc = queue.point((l, 4), dc)
    dc_low, dc_high = rims(dc)
    wide = pltpu.VMEM((rows + 2 * EDGE, D), F32)
    dx2, dheads, a2, dg, dy1, small_two = fused(
        conv_back_kernel,
        0,
        [dc, dc_low, dc_high, z, z_low, z_high, masks, taps, x2, dx3, glu, attn_out, gains],
        [
            stream,
            jax.ShapeDtypeStruct((HEADS, HD, rows), BF16),
            low,
            jax.ShapeDtypeStruct((rows, 2 * D), BF16),
            low,
            jax.ShapeDtypeStruct((KER + 1, D), F32),
        ],
        10 * rows * D * D,
        scratch=[wide, wide, pltpu.VMEM((KER, rows, 128), F32), pltpu.VMEM((rows, D), F32)],
    )
    dglu = dot(a2, dg, 0, 0).astype(BF16)
    dattn_out = dot(dy1, o, 0, 1).astype(BF16)
    early = [dglu, dattn_out, dconv_out]
    if l == 0:
        early_sums = []

        def through(arrays):
            parts = dense_both(early, arrays, flipped())
            parts = list(parts) if flipped() else [parts]
            queue.at((l, 7), parts, early_sums.extend)

        queue.at((l, 6), dense_other(early, flipped())[0], through)
    dheads = queue.point((l, 5), heads_grad(dheads))
    many = queries.shape[0] > 1
    dt = attend_back(
        spans if many else own_spans[None],
        rotary if many else own_rotary[None],
        rotary,
        queries,
        keys,
        1 if many else 0,
        dheads,
        full,
        log_total,
    )
    dt = [queue.point((l, 6), dt[0])] + list(dt[1:])
    dt = queue.point((l, 7), heads_back(dt))
    lead, (dqkv, dffn_in, dffn_out, small_three) = enter_back(
        below and below[4], dt, x1, x, dx2, qkv, ffn_in, ffn_out, gains, below and below[:4]
    )
    small = jnp.concatenate([small_one, small_two, small_three], axis=0)
    late = [dffn_in, dqkv, dffn_out]
    if l == 0:
        dense = (late, early_sums)
    else:
        dense = [dffn_in, dqkv, dglu, dffn_out, dattn_out, dconv_out]
    grads = lead[0] if below is None else (lead[0], lead[1], lead[2:])
    return grads, dense, expert_sums[0], small


def small_total(grad):
    groups = lax.axis_size(EXPERT)
    width = D // groups
    me = lax.axis_index(EXPERT)
    if flipped():
        pieces = [
            lax.dynamic_slice_in_dim(grad, (me ^ k) * width, width, axis=1) for k in range(groups)
        ]
    else:
        pieces = [grad[:, k * width : (k + 1) * width] for k in range(groups)]
    return summed_everywhere(summed(passed(pieces, EXPERT)), (HC, HX, DP))


def adamw(master, moment, square, gradient, rate, decay):
    moment_new = BETA_ONE * moment + (1.0 - BETA_ONE) * gradient
    square_new = BETA_TWO * square + (1.0 - BETA_TWO) * gradient * gradient
    unbiased = moment_new / (1.0 - BETA_ONE**STEP)
    scaled = square_new / (1.0 - BETA_TWO**STEP)
    updated = master - rate * (unbiased / (jnp.sqrt(scaled) + ADAM_EPS) + decay * master)
    return (updated, moment_new, square_new)


def expert_adamw_kernel(rates, pair, me, own_ref, other_ref, *refs):
    ins, outs = refs[:6], refs[-6:]
    grad = own_ref[...].astype(F32)
    if pair:
        grad = jnp.where(pl.program_id(0) == me[0], grad, other_ref[...].astype(F32))
    _, depth, width = grad.shape
    blocks = [grad[1, :, i : i + depth] for i in range(0, width, depth)]
    for k, value in enumerate((grad[0], jnp.concatenate(blocks, axis=0))):
        new = adamw(*[ins[3 * k + i][0, 0] for i in range(3)], value, rates[k], DECAY)
        for i in range(3):
            outs[3 * k + i][0, 0] = new[i]


def expert_adamw(l, both, states, rates, filled):
    pair = lax.axis_size(HC) == 2
    depth, width = both.shape[1], both.shape[2] // (2 if pair else 1)
    own = both[..., :width]
    other = swap(both[..., width:]) if pair else own
    me = jnp.reshape(lax.axis_index(HC), (1,)).astype(jnp.int32)
    grad = pl.BlockSpec((2, depth, width), lambda e, at: (0, 0, 0))
    specs = [pl.BlockSpec((1, 1) + s.shape[2:], lambda e, at: (l, e, 0, 0)) for s in states]
    kept = [] if filled is None else list(filled)
    return pl.pallas_call(
        functools.partial(expert_adamw_kernel, rates, pair),
        grid_spec=pltpu.PrefetchScalarGridSpec(
            num_scalar_prefetch=1,
            grid=(states[0].shape[1],),
            in_specs=[grad, grad] + specs + [pl.BlockSpec(memory_space=pl.ANY)] * len(kept),
            out_specs=specs,
        ),
        out_shape=[shaped(s.shape, F32) for s in states],
        input_output_aliases={3 + len(states) + i: i for i in range(len(kept))},
        compiler_params=pltpu.CompilerParams(vmem_limit_bytes=32 << 20),
        cost_estimate=pl.CostEstimate(
            flops=0, bytes_accessed=12 * sum(s.size for s in states) // LAYERS, transcendentals=0
        ),
    )(me, own, other, *[still(v) for v in states], *kept)


def on_device(
    frames,
    cotangent,
    lengths,
    routes,
    entry_weights,
    entry_moment,
    entry_square,
    exit_weights,
    exit_moment,
    exit_square,
    upward_weights,
    upward_moment,
    upward_square,
    downward_weights,
    downward_moment,
    downward_square,
    norm_gains,
    gains_moment,
    gains_square,
    conv_kernel,
    kernel_moment,
    kernel_square,
    router_weights,
    router_moment,
    router_square,
):
    small = jnp.concatenate(
        [norm_gains, conv_kernel, jnp.swapaxes(router_weights, 1, 2)], axis=1
    )
    if flipped():
        pieces = jnp.stack(passed([small] * 4, EXPERT))
        me = lax.axis_index(EXPERT)
        small = jnp.concatenate([take(pieces, 0, e ^ me) for e in range(4)], axis=2)
    else:
        small = lax.all_gather(small, EXPERT, axis=2, tiled=True)
    counts = (norm_gains.shape[1], conv_kernel.shape[1])
    x = to_frames(frames).astype(F32)
    upstream = to_frames(cotangent)
    tables = build_tables(lengths, routes, x.shape[0])
    shards, experts, queue = [], [], Queue()
    for l in range(LAYERS):
        shard = dense_shard(entry_weights[l], exit_weights[l])
        shards.append(shard)
        own = expert_shard(upward_weights[l], downward_weights[l])
        if l == 0 and flipped():
            experts.append([])
            queue.at((0, -1), passed([own] * 4, PLANE), experts[0].extend)
        else:
            experts.append(lax.all_gather(own, PLANE, axis=0, tiled=False))
    above = []
    queue.at((0, -1), [upstream], above.extend)
    saved, layer_weights, left = [], [], []
    for l in range(LAYERS):
        if l == 0 and flipped():
            shard = shards[0]
            first = jnp.concatenate([shard[0:4], shard[9:13]], axis=0)
            others = jnp.concatenate([shard[4:9], shard[13:15]], axis=0)
            (ffn_in, ffn_out), (x, small) = dense_gather_steps(first, (4, 4), [x, small])
            qkv, glu, attn_out, conv_out = dense_gather(others, (3, 2, 1, 1))
            dense = [ffn_in, qkv, glu, ffn_out, attn_out, conv_out]
        elif l == 0:
            dense = dense_gather(shards[0], UNITS)
        weights = tuple(dense) + (
            experts[l],
            small[l, : counts[0]],
            small[l, counts[0] : sum(counts)],
            small[l, sum(counts) :].astype(BF16),
        )
        layer_weights.append(weights)
        coming = shards[l + 1 : l + 2]
        kept, rest, dense = forward_layer(l, x, left[-1] if left else None, weights, tables, queue, coming)
        saved.append(kept)
        left.append(rest)

    rows = x.shape[0]
    x3, gate, halves, gains, part = left[-1]
    stream = jax.ShapeDtypeStruct((rows, D), F32)
    encoded, dx4, dgate, last_gain, *sent = fused(
        functools.partial(turn_kernel, len(halves)),
        part,
        [above[0], x3, gate, gains] + list(halves),
        [
            jax.ShapeDtypeStruct((rows, D), BF16),
            stream,
            jax.ShapeDtypeStruct((rows, 1), F32),
            jax.ShapeDtypeStruct((8, D), F32),
        ]
        + half_shapes(rows),
        0,
    )
    grads = (dx4, dgate, sent)
    wide_rate = 2.0 * D ** (-0.5)
    rates = (wide_rate, 2.0 * max(EFF // 64, 1) ** (-0.5))
    kernel_rate = 2.0 * KER ** (-0.5)
    states = (
        upward_weights, upward_moment, upward_square, downward_weights, downward_moment, downward_square
    )
    small_grads, dense_sums, expert_next = [last_gain], [None] * LAYERS, None
    for l in reversed(range(LAYERS)):
        below = left[l - 1] if l > 0 else None
        grads, dense, dexpert, small_grad = backward_layer(
            l, grads, layer_weights[l], saved[l], left[l], below, tables, queue
        )
        small_grads.insert(0, small_grad)
        if l > 0:
            expert_next = expert_adamw(l, dexpert, states, rates, expert_next)
            scatter_later(queue, l, dense, dense_sums)

            def update(arrays):
                nonlocal expert_next
                expert_next = arrays

            queue.at((l - 1, 7), expert_next, update)

    late, early = dense
    other, (grads, encoded, *small_grads) = dense_other(
        late, flipped(), [grads, encoded] + small_grads
    )
    small_grad = small_total(jnp.concatenate(small_grads, axis=0))
    early = passed(early if flipped() else early[0], PLANE)
    early = summed(dense_expert(early))
    late = passed(dense_both(late, other, flipped()), PLANE)
    both = from_frames(jnp.concatenate([encoded, grads], axis=0)).astype(F32)
    expert_next = expert_adamw(0, dexpert, states, rates, expert_next)
    late, others = tie(late, list(expert_next) + [both, early, small_grad] + dense_sums[1:])
    expert_next, (both, early, small_grad), dense_sums[1:] = others[:6], others[6:9], others[9:]
    encoded, input_gradient = both[:, : frames.shape[1]], both[:, frames.shape[1] :]
    gains_grad, kernel_grad, router_grad = small_sums(small_grad)
    late = summed(dense_expert(late))
    cut = [late[:7], early[:2], late[7:], early[2:]]
    dense_grad = jnp.stack([jnp.concatenate(cut, axis=0)] + [v.astype(F32) for v in dense_sums[1:]])
    entry_grad = jnp.swapaxes(dense_grad[:, 0:9], 1, 2)
    exit_grad = jnp.swapaxes(dense_grad[:, 9:], 2, 3)
    return (
        (encoded, input_gradient)
        + adamw(entry_weights, entry_moment, entry_square, entry_grad, wide_rate, DECAY)
        + adamw(exit_weights, exit_moment, exit_square, exit_grad, wide_rate, DECAY)
        + tuple(expert_next)
        + adamw(norm_gains, gains_moment, gains_square, gains_grad, 0.5, 0.0)
        + adamw(conv_kernel, kernel_moment, kernel_square, kernel_grad, kernel_rate, DECAY)
        + adamw(router_weights, router_moment, router_square, router_grad, wide_rate, DECAY)
    )


def scatter_later(queue, l, grads, sums):
    def sum_plane(arrays):
        queue.at((l - 1, 4), [dense_both(grads, arrays, False)], sum_parts)

    def sum_parts(arrays):
        part = lax.psum_scatter(arrays[0], PLANE, scatter_dimension=0, tiled=False)
        sum_expert([part])

    def sum_expert(arrays):
        sums[l] = lax.psum_scatter(arrays[0], EXPERT, scatter_dimension=0, tiled=False)

    def give(arrays):
        queue.at((l - 1, 3), [swap(piece) for piece in arrays], sum_plane)

    if lax.axis_size(HC) == 1:
        sum_plane([])
    else:
        queue.at((l - 1, 2), dense_pack(grads, 1 - lax.axis_index(HC), False, True), give)


def small_sums(total):
    each = 2 * EXPERTS + KER + 1 + 8
    gains, taps, routers = [], [], []
    for l in range(LAYERS):
        own = total[l * each : (l + 1) * each]
        over = (l + 1) * each + (each - 8 + 4 if l + 1 < LAYERS else 0)
        two, three = 2 * EXPERTS, 2 * EXPERTS + KER + 1
        gains.append(
            jnp.concatenate(
                [own[three : three + 2], own[three - 1 : three], own[EXPERTS : EXPERTS + 1], total[over : over + 1]]
            )
        )
        taps.append(own[two : two + KER])
        routers.append(own[:EXPERTS].T)
    return jnp.stack(gains), jnp.stack(taps), jnp.stack(routers)


def finer(mesh, bins):
    n_dp, n_expert, n_hidden = mesh.devices.shape
    each = bins // n_dp
    pair = EXPERTS // n_expert
    shape = (n_dp, each, n_expert // each, n_hidden // pair, pair)
    return Mesh(mesh.devices.reshape(shape), ALL)


def solution(mesh):
    hidden = (HX, HC)
    stream = P(DP, hidden, EXPERT)
    entry = P(None, (DP, HX, HC), None, EXPERT)
    leave = P(None, None, EXPERT, (DP, HX, HC))
    upward = P(None, EXPERT, DP, hidden)
    downward = P(None, EXPERT, hidden, DP)
    last = P(None, None, EXPERT)
    middle = P(None, EXPERT, None)
    states = sum([(s,) * 3 for s in (entry, leave, upward, downward, last, last, middle)], ())

    def program(*args):
        return jax.shard_map(
            on_device,
            mesh=finer(mesh, args[0].shape[0]),
            in_specs=(stream, stream, P(DP, None), P(DP, hidden, None)) + states,
            out_specs=(stream, stream) + states,
            check_vma=False,
        )(*args)

    return program
```

```python
import functools
import math

import jax
import jax.numpy as jnp
import numpy as np
from jax import lax
from jax.experimental import pallas as pl
from jax.experimental.pallas import tpu as pltpu
from jax.sharding import Mesh
from jax.sharding import PartitionSpec as P

D = 512
HEADS = 8
HD = 64
HALF = HD // 2
EFF = 2048
EXPERTS = 8
KER = 15
RIM = KER // 2
EDGE = 16
LARGE = 700 << 10
UNITS = (4, 3, 2, 4, 1, 1)
LAYERS = 2
STEP = 5
EPS = 1e-05
NEG = -1e30
BETA_ONE = 0.9
BETA_TWO = 0.98
ADAM_EPS = 1e-08
DECAY = 0.01
BEST = lax.Precision.HIGHEST
F32 = jnp.float32
BF16 = jnp.bfloat16

DP, EB, ES, HX, HC = "dp", "eb", "es", "hx", "hc"
ALL = (DP, EB, ES, HX, HC)
EXPERT = (EB, ES)
PLANE = (DP, HX)
MOE = (EB, ES, HC)


def paired():
    return lax.axis_size(HC) == lax.axis_size(ES)


def frame_axes():
    return (HX, ES, HC) if paired() else (HX, HC, ES)


def sub_axis():
    return HC if paired() else ES


def dot(left, right, left_dim, right_dim, **kw):
    return lax.dot_general(
        left, right, (((left_dim,), (right_dim,)), ((), ())), preferred_element_type=F32, **kw
    )


def swap(block):
    return lax.ppermute(block, HC, [(0, 1), (1, 0)])


def still(block):
    if block.size * block.dtype.itemsize < LARGE:
        return block
    return pltpu.with_memory_space_constraint(block, pltpu.HBM)


def shaped(shape, dtype):
    if math.prod(shape) * jnp.dtype(dtype).itemsize < LARGE:
        return jax.ShapeDtypeStruct(shape, dtype)
    return pltpu.HBM(shape, dtype)


def take(block, axis, index):
    return lax.dynamic_index_in_dim(block, index, axis, keepdims=False)


def stack_pair(own, other, axis):
    me = lax.axis_index(HC)
    return jnp.where(
        me == 0, jnp.stack([own, other], axis), jnp.stack([other, own], axis)
    )


def exchange(block, axes):
    return lax.all_to_all(block, axes, split_axis=0, concat_axis=0, tiled=True)


def flipped():
    return paired() and lax.axis_size(PLANE) == 4 and lax.axis_size(EXPERT) == 4


def flip(block, axes, k):
    return lax.ppermute(block, axes, [(i, i ^ k) for i in range(lax.axis_size(axes))])


def tie(value, others):
    value, others = lax.optimization_barrier((value, tuple(others)))
    return value, list(others)


class Queue:
    def __init__(self):
        self.marks = {}

    def at(self, mark, arrays, then):
        self.marks.setdefault(mark, []).append((list(arrays), then))

    def point(self, mark, value):
        for arrays, then in self.marks.pop(mark, []):
            value, arrays = tie(value, arrays)
            then(arrays)
        return value


def passed(pieces, axes):
    if flipped():
        return [pieces[0]] + [flip(pieces[k], axes, k) for k in range(1, len(pieces))]
    whole = exchange(jnp.stack(pieces) if isinstance(pieces, list) else pieces, axes)
    return [whole[k] for k in range(whole.shape[0])]


def summed(pieces):
    return functools.reduce(jnp.add, [p.astype(F32) for p in pieces])


def summed_everywhere(value, axes):
    for axis in axes:
        k = 1
        while k < lax.axis_size(axis):
            value = value + flip(value, axis, k)
            k *= 2
    return value


def to_frames(block):
    bins, rows, width = block.shape
    parts = lax.axis_size(sub_axis())
    block = block.reshape(bins, parts, rows // parts, width)
    if paired():
        me = lax.axis_index(HC)
        block = stack_pair(take(block, 1, me), swap(take(block, 1, 1 - me)), 1)
    block = exchange(block.reshape(bins * parts, rows // parts, width), EXPERT)
    return jnp.swapaxes(block, 0, 1).reshape(rows // parts, -1)


def from_frames(block):
    groups, parts = lax.axis_size(EXPERT), lax.axis_size(sub_axis())
    bins, width = groups // parts, D // groups
    runs = 2
    rows = block.shape[0] // runs
    block = jnp.swapaxes(block.reshape(runs * rows, groups, width), 0, 1)
    block = exchange(block, EXPERT).reshape(bins, parts, runs, rows, width)
    if paired():
        me = lax.axis_index(HC)
        block = stack_pair(take(block, 1, me), swap(take(block, 1, 1 - me)), 2)
    else:
        block = jnp.swapaxes(block, 1, 2)
    return block.reshape(bins, runs * parts * rows, width)


def feature_part(turned):
    me = lax.axis_index(HC)
    return me ^ lax.axis_index(DP) if turned else me


def dense_shard(entry, leave):
    entry = jnp.swapaxes(entry.astype(BF16), 0, 1)
    leave = jnp.swapaxes(leave.astype(BF16), 1, 2)
    return jnp.concatenate([entry, leave], axis=0)


def unpack_kernel(in_ref, *outs):
    _, groups, _, _, _, width = in_ref.shape
    at = 0
    for out in outs:
        for k in range(out.shape[1] // width):
            out[:, k * width : (k + 1) * width] = in_ref[0, k % groups, 0, at + k // groups]
        at += out.shape[1] // (width * groups)


def dense_collect(shard):
    n_dp, n_e, n_h = lax.axis_size(DP), lax.axis_size(EXPERT), lax.axis_size((HX, HC))
    whole = lax.all_gather(shard, ALL, axis=0, tiled=False)
    return whole.reshape((n_dp, n_e, n_h) + shard.shape)


def dense_unpack(whole, units):
    n_dp, n_e, n_h, count, rows, columns = whole.shape
    return pl.pallas_call(
        unpack_kernel,
        grid=(n_dp * n_h,),
        in_specs=[
            pl.BlockSpec(
                (1, n_e, 1, count, rows, columns), lambda r: (r // n_h, 0, r % n_h, 0, 0, 0)
            )
        ],
        out_specs=[pl.BlockSpec((rows, n * D), lambda r: (r, 0)) for n in units],
        out_shape=[shaped((D, n * D), BF16) for n in units],
        compiler_params=pltpu.CompilerParams(vmem_limit_bytes=32 << 20),
        cost_estimate=pl.CostEstimate(
            flops=0, bytes_accessed=4 * count * D * D, transcendentals=0
        ),
    )(still(whole))


def dense_gather(shard, units):
    return dense_unpack(dense_collect(shard), units)


def unpack_steps_kernel(base, *refs):
    pieces, outs = refs[:8], refs[8:]
    own, other = pieces[:4], pieces[4:]
    groups, _, rows, width = own[0].shape

    def fill(k):
        for arrays, core in ((own, base[0]), (other, 1 - base[0])):
            place, at = pl.ds(pl.multiple_of(core * rows, rows), rows), 0
            for out in outs:
                for u in range(out.shape[1] // D):
                    for e in range(groups):
                        column = pl.multiple_of(u * D + (e ^ base[2]) * width, width)
                        out[place, pl.ds(column, width)] = arrays[k][e, at + u]
                at += out.shape[1] // D

    for k in range(4):
        pl.when(pl.program_id(0) == k)(functools.partial(fill, k))


def dense_gather_steps(shard, units, ahead):
    count, rows, columns = shard.shape
    wide = jnp.stack(passed([shard] * 4, EXPERT))
    own = passed([wide] * 4, PLANE)
    own[1], ahead = tie(own[1], ahead)
    other = [swap(piece) for piece in own]
    base = [lax.axis_index(a) for a in (HC, PLANE, EXPERT)]
    whole = pl.BlockSpec(wide.shape, lambda k, at: (0, 0, 0, 0))
    out = pl.pallas_call(
        unpack_steps_kernel,
        grid_spec=pltpu.PrefetchScalarGridSpec(
            num_scalar_prefetch=1,
            grid=(4,),
            in_specs=[whole] * 8,
            out_specs=[pl.BlockSpec((2 * rows, n * D), lambda k, at: (k ^ at[1], 0)) for n in units],
        ),
        out_shape=[shaped((D, n * D), BF16) for n in units],
        compiler_params=pltpu.CompilerParams(vmem_limit_bytes=40 << 20),
        cost_estimate=pl.CostEstimate(
            flops=0, bytes_accessed=4 * count * D * D, transcendentals=0
        ),
    )(jnp.stack(base), *own, *other)
    return out, ahead


def pack_kernel(count, extra, base, *refs):
    grads, added, outs = refs[:count], refs[count : count + extra], refs[count + extra :]
    groups, width = outs[0].shape[-4], outs[0].shape[-1]

    def fill(out, head, other):
        at = 0
        for ref in grads:
            for k in range(ref.shape[1] // width):
                piece = ref[:, k * width : (k + 1) * width]
                e, place = (k % groups) ^ base[2], at + k // groups
                if other is not None:
                    piece = (piece.astype(F32) + other[e, place].astype(F32)).astype(BF16)
                out[head + (e, place)] = piece
            at += ref.shape[1] // (width * groups)

    if len(outs) == 1 and not extra:
        fill(outs[0], (0,), None)
        return
    for p in range(max(len(outs), extra)):
        out, head = (outs[0], (0,)) if len(outs) == 1 else (outs[p], ())
        pl.when(pl.program_id(0) == p)(functools.partial(fill, out, head, added[p] if extra else None))


def dense_pack(grads, core, turned, listed, added=()):
    n_e, n_p, n_c = lax.axis_size(EXPERT), lax.axis_size(PLANE), lax.axis_size(HC)
    count = sum(g.shape[1] for g in grads) // D
    rows, columns = D // (n_p * n_c), D // n_e
    shape = (n_p, n_e, count, rows, columns)
    base = [core] + [lax.axis_index(a) if turned else 0 for a in (PLANE, EXPERT)]
    piece = pl.BlockSpec((1,) + shape[1:], lambda p, at: (p, 0, 0, 0, 0))
    whole = pl.BlockSpec(shape[1:], lambda p, at: (0, 0, 0, 0))
    specs = [
        pl.BlockSpec((rows, g.shape[1]), lambda p, at: ((p ^ at[1]) * n_c + at[0], 0)) for g in grads
    ]
    out = pl.pallas_call(
        functools.partial(pack_kernel, len(grads), len(added)),
        grid_spec=pltpu.PrefetchScalarGridSpec(
            num_scalar_prefetch=1,
            grid=(n_p,),
            in_specs=specs + [whole] * len(added),
            out_specs=[whole] * n_p if listed else piece,
        ),
        out_shape=[shaped(shape[1:], BF16)] * n_p if listed else shaped(shape, BF16),
        compiler_params=pltpu.CompilerParams(vmem_limit_bytes=40 << 20),
        cost_estimate=pl.CostEstimate(
            flops=0, bytes_accessed=4 * count * D * D // n_c, transcendentals=0
        ),
    )(
        jnp.stack([jnp.asarray(b, jnp.int32) for b in base]),
        *[still(v) for v in list(grads) + list(added)],
    )
    return list(out) if listed else out


def dense_other(grads, turned, after=()):
    if lax.axis_size(HC) == 1:
        return [], list(after)
    pieces, after = tie(dense_pack(grads, 1 - lax.axis_index(HC), turned, True), after)
    return [swap(piece) for piece in pieces], after


def dense_both(grads, other, turned):
    core = lax.axis_index(HC) if other else 0
    return dense_pack(grads, core, turned, turned, other)


def expert_shard(up, down):
    up, down = up.astype(BF16), down.astype(BF16)
    depth = up.shape[1]
    down = down.reshape(down.shape[0], -1, depth, depth).swapaxes(1, 2).reshape(up.shape)
    both = jnp.stack([up, down], axis=1)
    if lax.axis_size(HC) == 1:
        return both[0]
    me = lax.axis_index(HC)
    return jnp.concatenate([take(both, 0, me), swap(take(both, 0, 1 - me))], axis=2)


def gather_rows(in_ref, out, parts):
    _, capacity, width = in_ref.shape
    for i in range(in_ref.shape[0]):
        g, p = i // parts, i % parts
        out[g * capacity : (g + 1) * capacity, p * width : (p + 1) * width] = in_ref[i]


def part_rows(value, out_ref, parts):
    _, capacity, width = out_ref.shape
    for i in range(out_ref.shape[0]):
        g, p = i // parts, i % parts
        rows = value[g * capacity : (g + 1) * capacity, p * width : (p + 1) * width]
        out_ref[i] = rows.astype(out_ref.dtype)


def expert_kernel(parts, n_dp, base, x_ref, *refs):
    weights, (y_ref, x, y) = refs[:-3], refs[-3:]
    _, _, depth, width = weights[0].shape
    step, each = pl.program_id(0), len(weights) // n_dp

    @pl.when(step == 0)
    def _():
        gather_rows(x_ref, x, parts)
        y[...] = jnp.zeros_like(y)

    cuts = [slice(i * depth, (i + 1) * depth) for i in range(n_dp)]
    blocks = [slice(i, i + depth) for i in range(0, width, depth)]
    for n in range(each):
        own = [weights[i * each + n] for i in range(n_dp)]
        u = sum(contract(x[:, cuts[i]], own[i][0, 0], 1, 0) for i in range(n_dp))
        hidden = (u * jax.nn.sigmoid(u)).astype(BF16)
        for i in range(n_dp):
            y[:, cuts[i]] += sum(contract(hidden[:, b], own[i][0, 1, :, b], 1, 0) for b in blocks)

    @pl.when(step == pl.num_programs(0) - 1)
    def _():
        part_rows(y[...], y_ref, parts)


def expert_back_kernel(parts, n_dp, base, x_ref, g_ref, *refs):
    weights, (dx_ref, dw_ref, x, g, dx) = refs[:-5], refs[-5:]
    _, _, depth, width = weights[0].shape
    step, each = pl.program_id(0), len(weights) // n_dp

    @pl.when(step == 0)
    def _():
        gather_rows(x_ref, x, parts)
        gather_rows(g_ref, g, parts)
        dx[...] = jnp.zeros_like(dx)

    cuts = [slice(i * depth, (i + 1) * depth) for i in range(n_dp)]
    blocks = [slice(i, i + depth) for i in range(0, width, depth)]
    for n in range(each):
        own = [weights[i * each + n] for i in range(n_dp)]
        u = sum(contract(x[:, cuts[i]], own[i][0, 0], 1, 0) for i in range(n_dp))
        logistic = jax.nn.sigmoid(u)
        hidden = (u * logistic).astype(BF16)
        dh = [sum(contract(g[:, cuts[i]], own[i][0, 1, :, b], 1, 1) for i in range(n_dp)) for b in blocks]
        dh = jnp.concatenate(dh, axis=1)
        du = (dh * (logistic * (1.0 + u * (1.0 - logistic)))).astype(BF16)
        for i in range(n_dp):
            at = (i * each + n) ^ base[0]
            dw_ref[at, 0] = contract(x[:, cuts[i]], du, 0, 0).astype(BF16)
            for b in blocks:
                dw_ref[at, 1, :, b] = contract(hidden[:, b], g[:, cuts[i]], 0, 0).astype(BF16)
            dx[:, cuts[i]] += contract(du, own[i][0, 0], 1, 1)

    @pl.when(step == pl.num_programs(0) - 1)
    def _():
        part_rows(dx[...], dx_ref, parts)


def expert_call(pieces, weights, grads=None):
    parts = D // pieces.shape[2]
    n_dp, count = lax.axis_size(DP), lax.axis_size(PLANE)
    turned = isinstance(weights, list)
    arrays = [w[None] for w in weights] if turned else [weights] * count
    _, _, depth, width = arrays[0].shape
    cut = min(width, 512)
    rows = pieces.size // D
    base = jnp.reshape(lax.axis_index(PLANE) if turned else jnp.int32(0), (1,)).astype(jnp.int32)
    whole = pl.BlockSpec(pieces.shape, lambda c, at: (0, 0, 0))
    slabs = [
        pl.BlockSpec((1, 2, depth, cut), lambda c, at, k=0 if turned else k: (k, 0, 0, c))
        for k in range(count)
    ]
    shape = jax.ShapeDtypeStruct(pieces.shape, BF16)
    kept = pltpu.VMEM((rows, D), BF16)
    if grads is None:
        return pl.pallas_call(
            functools.partial(expert_kernel, parts, n_dp),
            grid_spec=pltpu.PrefetchScalarGridSpec(
                num_scalar_prefetch=1,
                grid=(width // cut,),
                in_specs=[whole] + slabs,
                out_specs=whole,
                scratch_shapes=[kept, pltpu.VMEM((rows, D), F32)],
            ),
            out_shape=shape,
            compiler_params=pltpu.CompilerParams(vmem_limit_bytes=40 << 20),
            cost_estimate=pl.CostEstimate(
                flops=4 * rows * D * EFF, bytes_accessed=4 * D * EFF, transcendentals=rows * EFF
            ),
        )(base, pieces, *[still(a) for a in arrays])
    return pl.pallas_call(
        functools.partial(expert_back_kernel, parts, n_dp),
        grid_spec=pltpu.PrefetchScalarGridSpec(
            num_scalar_prefetch=1,
            grid=(width // cut,),
            in_specs=[whole, whole] + slabs,
            out_specs=[whole, pl.BlockSpec((count, 2, depth, cut), lambda c, at: (0, 0, 0, c))],
            scratch_shapes=[kept, kept, pltpu.VMEM((rows, D), F32)],
        ),
        out_shape=[shape, shaped((count, 2, depth, width), BF16)],
        compiler_params=pltpu.CompilerParams(vmem_limit_bytes=40 << 20),
        cost_estimate=pl.CostEstimate(
            flops=12 * rows * D * EFF, bytes_accessed=8 * D * EFF, transcendentals=rows * EFF
        ),
    )(base, pieces, grads, *[still(a) for a in arrays])


def rotate(value, cosine, sine):
    low, high = value[..., :HALF, :], value[..., HALF:, :]
    return jnp.concatenate([low * cosine - high * sine, low * sine + high * cosine], axis=-2)


def unrotate(value, cosine, sine):
    low, high = value[..., :HALF, :], value[..., HALF:, :]
    return jnp.concatenate([low * cosine + high * sine, high * cosine - low * sine], axis=-2)


def contract(left, right, left_dim, right_dim):
    return lax.dot_general(
        left, right, (((left_dim,), (right_dim,)), ((), ())), preferred_element_type=F32
    )


def masked_scores(raw, low, high, base):
    place = base + lax.broadcasted_iota(jnp.int32, raw.shape, 0)
    return jnp.where((place >= low) & (place < high), raw, NEG)


def attend_kernel(unroll, span_ref, q_ref, k_ref, v_ref, o_ref, full_ref, lse_ref, scratch):
    count, width = k_ref.shape[0], k_ref.shape[-1]

    def one(j, _):
        low, high = span_ref[j, 0:1], span_ref[j, 1:2]
        query, scores = q_ref[j, 0, 0], scratch.at[j % unroll]
        peak = None
        for i in range(count):
            part = masked_scores(contract(k_ref[i, 0, 0], query, 0, 0), low, high, i * width)
            scores[i] = part
            top = jnp.max(part, axis=0, keepdims=True)
            peak = top if peak is None else jnp.maximum(peak, top)
        total = jnp.zeros_like(peak)
        mixed = jnp.zeros(query.shape, F32)
        for i in range(count):
            part = jnp.exp(scores[i] - peak)
            total = total + jnp.sum(part, axis=0, keepdims=True)
            mixed = mixed + contract(v_ref[i, 0, 0], part.astype(BF16), 1, 0)
        mixed = mixed * (1.0 / total)
        o_ref[j, 0] = mixed.astype(BF16)
        full_ref[j, 0] = mixed
        lse_ref[j, 0] = peak + jnp.log(total)
        return 0

    lax.fori_loop(0, q_ref.shape[0], one, 0, unroll=unroll)


def attend_back_kernel(
    unroll, together, span_ref, rot_q, rot_k, q_ref, k_ref, v_ref, g_ref, full_ref, lse_ref, *refs
):
    dk, dv, kt, vt = refs[-4:]
    dkv_ref, base = refs[-5], 1 if together else 0
    count, width = k_ref.shape[0], k_ref.shape[-1]
    dk[...] = jnp.zeros_like(dk)
    dv[...] = jnp.zeros_like(dv)
    for i in range(count):
        kt[i] = k_ref[i, 0, 0].T
        vt[i] = v_ref[i, 0, 0].T

    def one(j, _):
        low, high = span_ref[j, 0:1], span_ref[j, 1:2]
        query, grad, log_total = q_ref[j, 0, 0], g_ref[j, 0], lse_ref[j, 0]
        query_turned, grad_turned = query.T, grad.T
        delta = jnp.sum(grad.astype(F32) * full_ref[j, 0], axis=0, keepdims=True)

        def slopes(i):
            raw = masked_scores(contract(kt[i], query, 1, 0), low, high, i * width)
            part = jnp.exp(raw - log_total)
            slope = part * (contract(vt[i], grad, 1, 0) - delta)
            return part.astype(BF16), slope.astype(BF16)

        dq = jnp.zeros(query.shape, F32)
        coming = slopes(0)
        for i in range(count):
            part, slope = coming
            if i + 1 < count:
                coming = slopes(i + 1)
            dv[i] += contract(part, grad_turned, 1, 0)
            dk[i] += contract(slope, query_turned, 1, 0)
            dq = dq + contract(k_ref[i, 0, 0], slope, 1, 0)
        dq = unrotate(dq * HD ** (-0.5), rot_q[j, 0], rot_q[j, 1]).astype(BF16)
        if together:
            dkv_ref[j, 0, 0] = dq
        else:
            refs[0][j, 0] = dq
        return 0

    lax.fori_loop(0, q_ref.shape[0], one, 0, unroll=unroll)
    for i in range(count):
        dkv_ref[i, base, 0] = unrotate(dk[i].T, rot_k[i, 0], rot_k[i, 1]).astype(BF16)
        dkv_ref[i, base + 1, 0] = dv[i].T.astype(BF16)


def head_spec(block, part=None):
    if part is None:
        shape = (block.shape[0], 1) + block.shape[2:]
        return pl.BlockSpec(shape, lambda h: (0, h, 0, 0))
    shape = (block.shape[0], 1, 1) + block.shape[3:]
    return pl.BlockSpec(shape, lambda h: (0, part, h, 0, 0))


def attend(spans, queries, keys, first):
    nq, _, heads, _, width = queries.shape
    nk, unroll = keys.shape[0], min(4, nq)
    outs = [
        jax.ShapeDtypeStruct((nq, heads, HD, width), BF16),
        jax.ShapeDtypeStruct((nq, heads, HD, width), F32),
        jax.ShapeDtypeStruct((nq, heads, 1, width), F32),
    ]
    return pl.pallas_call(
        functools.partial(attend_kernel, unroll),
        grid=(heads,),
        in_specs=[
            pl.BlockSpec(spans.shape, lambda h: (0, 0, 0)),
            head_spec(queries, 0),
            head_spec(keys, first),
            head_spec(keys, first + 1),
        ],
        out_specs=[head_spec(o) for o in outs],
        out_shape=outs,
        scratch_shapes=[pltpu.VMEM((unroll, nk, width, width), F32)],
        compiler_params=pltpu.CompilerParams(vmem_limit_bytes=40 << 20),
        cost_estimate=pl.CostEstimate(
            flops=4 * heads * nq * nk * width * width * HD,
            bytes_accessed=4 * heads * (nq + nk) * HD * width,
            transcendentals=heads * nq * nk * width * width,
        ),
    )(spans, queries, keys, keys)


def attend_back(spans, rot_q, rot_k, queries, keys, first, grads, full, log_total):
    nq, _, heads, _, width = queries.shape
    nk = keys.shape[0]
    together = nq == nk
    outs = [jax.ShapeDtypeStruct((nk, 3 if together else 2, heads, HD, width), BF16)]
    out_specs = [pl.BlockSpec(outs[0].shape[:2] + (1, HD, width), lambda h: (0, 0, h, 0, 0))]
    if not together:
        outs.insert(0, jax.ShapeDtypeStruct((nq, heads, HD, width), BF16))
        out_specs.insert(0, head_spec(outs[0]))
    whole = lambda v: pl.BlockSpec(v.shape, lambda h: (0,) * len(v.shape))
    return pl.pallas_call(
        functools.partial(attend_back_kernel, min(2, nq), together),
        grid=(heads,),
        in_specs=[
            whole(spans),
            whole(rot_q),
            whole(rot_k),
            head_spec(queries, 0),
            head_spec(keys, first),
            head_spec(keys, first + 1),
            head_spec(grads),
            head_spec(full),
            head_spec(log_total),
        ],
        out_specs=out_specs,
        out_shape=outs,
        scratch_shapes=[pltpu.VMEM((nk, width, HD), F32)] * 2 + [pltpu.VMEM((nk, width, HD), BF16)] * 2,
        compiler_params=pltpu.CompilerParams(vmem_limit_bytes=40 << 20),
        cost_estimate=pl.CostEstimate(
            flops=10 * heads * nq * nk * width * width * HD,
            bytes_accessed=8 * heads * (nq + nk) * HD * width,
            transcendentals=heads * nq * nk * width * width,
        ),
    )(spans, rot_q, rot_k, queries, keys, keys, grads, full, log_total)


def build_tables(lengths, routes, rows):
    axes = frame_axes()
    total = rows * lax.axis_size(axes)
    order = lax.axis_index(axes)
    lengths = take(lengths, 0, lax.axis_index(EB))
    ends = jnp.cumsum(lengths)
    starts = ends - lengths
    places = jnp.arange(total, dtype=jnp.int32)
    segment = jnp.sum((places[:, None] >= ends[None, :]).astype(jnp.int32), axis=-1)
    member = segment[:, None] == jnp.arange(lengths.shape[0], dtype=jnp.int32)
    low = jnp.sum(jnp.where(member, starts, 0), axis=-1)
    high = jnp.sum(jnp.where(member, ends, 0), axis=-1)
    spans = jnp.stack([low, high]).reshape(2, -1, rows).swapaxes(0, 1)
    position = (places - low).reshape(-1, 1, rows)
    frequency = 10000.0 ** (-jnp.arange(HALF, dtype=F32) * 2.0 / HD)
    angles = position.astype(F32) * frequency[:, None]
    rotary = jnp.stack([jnp.cos(angles), jnp.sin(angles)], axis=1)
    wide = jnp.pad(segment, (RIM, RIM), constant_values=-1)
    wide = lax.dynamic_slice_in_dim(wide, order * rows, rows + 2 * RIM)
    own = wide[RIM : RIM + rows]
    masks = jnp.stack([(wide[i : i + rows] == own).astype(F32) for i in range(KER)], axis=1)

    routes = routes[..., 0]
    if paired():
        mine = lax.axis_index(HC) == lax.axis_index(ES)
        other = swap(routes)
        routes = jnp.where(mine, routes, other)
    chosen = take(routes, 0, lax.axis_index(EB))
    block = chosen.shape[0]
    capacity = 3 * block // 16
    experts = jnp.arange(EXPERTS, dtype=jnp.int32)
    onehot = chosen[:, None] == experts
    earlier = jnp.tril(jnp.ones((block, block), BF16), -1)
    slots = jnp.sum(jnp.where(onehot, dot(earlier, onehot.astype(BF16), 1, 0), 0.0), axis=-1)
    slots = slots.astype(jnp.int32)
    parts = lax.axis_size(sub_axis())
    sub = lax.axis_index(sub_axis())
    own_chosen = take(chosen.reshape(parts, -1), 0, sub)
    if paired():
        flip = lambda v: jnp.where(sub == 0, v, jnp.roll(v, block // 2))
        chosen, slots = flip(chosen), flip(slots)
    place = chosen * capacity + slots
    table = (jnp.arange(EXPERTS * capacity, dtype=jnp.int32)[:, None] == place).astype(BF16)
    if paired():
        table = (table[:, : block // 2], table[:, block // 2 :])
    own_onehot = (own_chosen[:, None] == experts).astype(F32)
    return spans, rotary, take(rotary, 0, order), take(spans, 0, order), masks, table, own_onehot


def rims(block):
    axes = (ES, HX, HC)
    sizes = [lax.axis_size(axis) for axis in axes]
    order = np.arange(math.prod(sizes)).reshape(sizes)
    order = [int(i) for i in np.transpose(order, [axes.index(a) for a in frame_axes()]).flat]
    low = lax.ppermute(block[-EDGE:], axes, list(zip(order[:-1], order[1:])))
    high = lax.ppermute(block[:EDGE], axes, list(zip(order[1:], order[:-1])))
    return low, high


def to_experts(halves, table):
    if paired():
        own, other = halves[0], swap(halves[1])
        sent = (dot(table[0], own, 1, 0) + dot(table[1], other, 1, 0)).astype(BF16)
    else:
        wide = lax.all_to_all(halves[0], ES, split_axis=1, concat_axis=0, tiled=True)
        sent = dot(table, wide, 1, 0).astype(BF16)
    return exchange(sent.reshape(EXPERTS, -1, sent.shape[1]), MOE)


def from_experts(pieces, table):
    got = exchange(pieces, MOE).reshape(EXPERTS * pieces.shape[1], -1)
    if paired():
        other = swap(dot(table[1], got, 0, 0).astype(BF16))
        return dot(table[0], got, 0, 0).astype(BF16), other
    return (lax.all_to_all(dot(table, got, 0, 0).astype(BF16), ES, split_axis=0, concat_axis=1, tiled=True),)


def heads_apart(block):
    if lax.axis_size(frame_axes()) == HEADS:
        got = exchange(block, frame_axes())[:, :, None]
        return got, got, 1
    block = jnp.swapaxes(block, 0, 1)
    return block[None, :1], lax.all_gather(block[1:], frame_axes(), axis=0, tiled=False), 0


def heads_together(block):
    if lax.axis_size(frame_axes()) == HEADS:
        block = exchange(block, frame_axes())
    return block.reshape(HEADS * HD, -1)


def heads_grad(block):
    if lax.axis_size(frame_axes()) == HEADS:
        return exchange(block, frame_axes())[:, None]
    return block[None]


def heads_back(grads):
    if len(grads) == 1:
        return exchange(grads[0][:, :, 0], frame_axes())
    dq, dkv = grads
    dkv = lax.psum_scatter(dkv, frame_axes(), scatter_dimension=0, tiled=False)
    return jnp.swapaxes(jnp.concatenate([dq, dkv], axis=0), 0, 1)


def unit(value):
    return lax.rsqrt(jnp.mean(value * value, axis=-1, keepdims=True) + EPS)


def normed(value, gain):
    return (value * unit(value) * gain).astype(BF16)


def norm_back(upstream, value, gain):
    factor = unit(value)
    gain_grad = jnp.sum(upstream * value * factor, axis=0, keepdims=True)
    scaled = gain * upstream
    mixed = jnp.sum(scaled * value, axis=-1, keepdims=True)
    return factor * scaled - value * (factor**3 * mixed / D), gain_grad


def joined(part, halves):
    if len(halves) == 1:
        return halves[0][...].astype(F32)
    own, other = halves[0][...].astype(F32), halves[1][...].astype(F32)
    first = part == 0
    return jnp.concatenate([jnp.where(first, own, other), jnp.where(first, other, own)], axis=1)


def give_halves(part, value, refs):
    if len(refs) == 1:
        refs[0][...] = value
        return
    low, high = value[:, : D // 2], value[:, D // 2 :]
    first = part == 0
    refs[0][...] = jnp.where(first, low.astype(F32), high.astype(F32)).astype(BF16)
    refs[1][...] = jnp.where(first, high.astype(F32), low.astype(F32)).astype(BF16)


def half_shapes(rows):
    count = 2 if paired() else 1
    return [jax.ShapeDtypeStruct((rows, D // count), BF16)] * count


def fused(kernel, scalar, args, out_shape, flops, grid=(), in_specs=None, out_specs=None, scratch=()):
    whole = lambda v: pl.BlockSpec(v.shape, lambda *at, n=len(v.shape): (0,) * n)
    in_specs = [spec or whole(a) for spec, a in zip(in_specs or [None] * len(args), args)]
    out_specs = [spec or whole(o) for spec, o in zip(out_specs or [None] * len(out_shape), out_shape)]
    size = sum(math.prod(v.shape) * v.dtype.itemsize for v in list(args) + list(out_shape))
    return pl.pallas_call(
        kernel,
        grid_spec=pltpu.PrefetchScalarGridSpec(
            num_scalar_prefetch=1,
            grid=grid or (1,),
            in_specs=in_specs,
            out_specs=out_specs,
            scratch_shapes=list(scratch),
        ),
        out_shape=out_shape,
        compiler_params=pltpu.CompilerParams(vmem_limit_bytes=56 << 20),
        cost_estimate=pl.CostEstimate(flops=flops, bytes_accessed=size, transcendentals=0),
    )(jnp.reshape(jnp.asarray(0 if scalar is None else scalar, jnp.int32), (1,)), *[still(a) for a in args])


def enter_kernel(halves, part, *refs):
    if halves:
        x3, gate, below = refs[:3]
        backs, refs = refs[3 : 3 + halves], refs[3 + halves :]
        gains, wi, wo, qkv, rot, x_ref, x1_ref, t_ref, a0, y = refs
    else:
        x_ref, gains, wi, wo, qkv, rot, x1_ref, t_ref, a0, y = refs
    step = pl.program_id(0)

    @pl.when(step == 0)
    def _():
        if halves:
            x4 = x3[...] + 0.5 * gate[...] * joined(part[0], backs)
            x_ref[...] = x4 * unit(x4) * below[4:5]
        a0[...] = normed(x_ref[...], gains[0:1])
        y[...] = jnp.zeros_like(y)

    u = contract(a0[...], wi[...], 1, 0)
    y[...] += contract((u * jax.nn.sigmoid(u)).astype(BF16), wo[...], 1, 1)

    @pl.when(step == pl.num_programs(0) - 1)
    def _():
        x1 = x_ref[...] + 0.5 * y[...]
        x1_ref[...] = x1
        t = contract(normed(x1, gains[1:2]), qkv[...], 1, 0).T
        cosine, sine = rot[0], rot[1]
        for h in range(HEADS):
            own = [t[w * D + h * HD : w * D + (h + 1) * HD] for w in range(3)]
            t_ref[h, 0] = (rotate(own[0], cosine, sine) * HD ** (-0.5)).astype(BF16)
            t_ref[h, 1] = rotate(own[1], cosine, sine).astype(BF16)
            t_ref[h, 2] = own[2].astype(BF16)


def enter(part, x, below, gains, ffn_in, ffn_out, qkv, rot):
    rows = (x if below is None else below[0]).shape[0]
    steps = ffn_in.shape[1] // D
    column = pl.BlockSpec((D, D), lambda j, at: (0, j))
    stream = jax.ShapeDtypeStruct((rows, D), F32)
    heads = jax.ShapeDtypeStruct((HEADS, 3, HD, rows), BF16)
    own = [gains, ffn_in, ffn_out, qkv, rot]
    if below is None:
        lead, outs = [x], [stream, heads]
    else:
        x3, gate, halves, above = below
        lead, outs = [x3, gate, above] + list(halves), [stream, stream, heads]
    out = fused(
        functools.partial(enter_kernel, 0 if below is None else len(below[2])),
        part,
        lead + own,
        outs,
        2 * rows * D * (2 * ffn_in.shape[1] + 3 * D),
        grid=(steps,),
        in_specs=[None] * len(lead) + [None, column, column, None, None],
        scratch=[pltpu.VMEM((rows, D), BF16), pltpu.VMEM((rows, D), F32)],
    )
    return (x,) + tuple(out) if below is None else tuple(out)


def middle_kernel(part, x1, o, attn_out, glu, gains, x2_ref, z_ref):
    x2 = x1[...] + contract(o[...], attn_out[...], 0, 1)
    x2_ref[...] = x2
    g = contract(normed(x2, gains[2:3]), glu[...], 1, 0)
    z_ref[...] = (g[:, :D] * jax.nn.sigmoid(g[:, D:])).astype(BF16)


def fill_wide(wide, low, block, high):
    rows = block.shape[0]
    wide[0:EDGE] = low[...].astype(F32)
    wide[EDGE : EDGE + rows] = block[...].astype(F32)
    wide[EDGE + rows :] = high[...].astype(F32)


def fill_masks(valid, masks):
    for i in range(KER):
        valid[i] = jnp.broadcast_to(masks[:, i : i + 1], valid.shape[1:])


def tiles(rows):
    size = min(rows, 64)
    return [(r, c, size) for c in range(0, D, 128) for r in range(0, rows, size)]


def conv_kernel_body(
    halves, part, x2, z, low, high, masks, taps, conv_out, gains, router, onehot, *refs
):
    x3_ref, c_ref, gate_ref = refs[:3]
    gives, wide, valid = refs[3 : 3 + halves], refs[-2], refs[-1]
    fill_wide(wide, low, z, high)
    fill_masks(valid, masks)
    for r, c, size in tiles(z.shape[0]):
        total = jnp.zeros((size, 128), F32)
        for i in range(KER):
            first = r + i + EDGE - RIM
            term = wide[first : first + size, c : c + 128] * valid[i, r : r + size]
            total = total + taps[i : i + 1, c : c + 128] * term
        c_ref[r : r + size, c : c + 128] = total
    mixed = c_ref[...]
    e = (mixed * jax.nn.sigmoid(mixed)).astype(BF16)
    x3 = x2[...] + contract(e, conv_out[...], 1, 1)
    x3_ref[...] = x3
    a3 = normed(x3, gains[3:4])
    gate_ref[...] = jnp.sum(softmax(contract(a3, router[...], 1, 1)) * onehot[...], axis=-1, keepdims=True)
    give_halves(part[0], a3, gives)


def softmax(logits):
    grown = jnp.exp(logits - jnp.max(logits, axis=-1, keepdims=True))
    return grown / jnp.sum(grown, axis=-1, keepdims=True)


def turn(upstream, x3, gate, back, gain):
    x4 = x3 + 0.5 * gate * back
    dx4, gain_grad = norm_back(upstream, x4, gain)
    half = 0.5 * dx4
    dgate = jnp.sum(half * back, axis=-1, keepdims=True)
    return x4, dx4, dgate, (gate * half).astype(BF16), gain_grad


def turn_kernel(halves, part, upstream, x3, gate, gains, *refs):
    backs, (out_ref, dx4_ref, dgate_ref, small_ref), gives = refs[:halves], refs[halves : halves + 4], refs[halves + 4 :]
    x4, dx4, dgate, sent, gain_grad = turn(
        upstream[...].astype(F32), x3[...], gate[...], joined(part[0], backs), gains[4:5]
    )
    out_ref[...] = (x4 * unit(x4) * gains[4:5]).astype(BF16)
    dx4_ref[...] = dx4
    dgate_ref[...] = dgate
    small_ref[...] = jnp.broadcast_to(gain_grad, small_ref.shape)
    give_halves(part[0], sent, gives)


def experts_back_kernel(
    halves, part, dx4, dgate, x3, mixed, gains, router, onehot, conv_out, *refs
):
    backs, (dx3_ref, dc_ref, dy2_ref, e_ref, small_ref) = refs[:halves], refs[halves:]
    a3 = normed(x3[...], gains[3:4])
    probs = softmax(contract(a3, router[...], 1, 1))
    gate = jnp.sum(probs * onehot[...], axis=-1, keepdims=True)
    dlogits = dgate[...] * probs * (onehot[...] - gate)
    wide = lambda a, b, i, j: lax.dot_general(
        a, b, (((i,), (j,)), ((), ())), preferred_element_type=F32, precision=BEST
    )
    da3 = joined(part[0], backs) + wide(dlogits, router[...].astype(F32), 1, 0)
    dn, gain_grad = norm_back(da3, x3[...], gains[3:4])
    dx3 = dx4[...] + dn
    dx3_ref[...] = dx3
    dy2 = dx3.astype(BF16)
    c = mixed[...]
    logistic = jax.nn.sigmoid(c)
    dy2_ref[...] = dy2
    e_ref[...] = (c * logistic).astype(BF16)
    slope = logistic * (1.0 + c * (1.0 - logistic))
    dc_ref[...] = (contract(dy2, conv_out[...], 1, 0) * slope).astype(BF16)
    small_ref[0:EXPERTS] = wide(dlogits, a3.astype(F32), 0, 0)
    small_ref[EXPERTS : 2 * EXPERTS] = jnp.broadcast_to(gain_grad, (EXPERTS, D))


def conv_back_kernel(
    part, dc, dlow, dhigh, z, low, high, masks, taps, x2, dx3, glu, attn_out, gains,
    dx2_ref, do_ref, a2_ref, dg_ref, dy1_ref, small_ref, wide, dwide, valid, dz,
):
    fill_wide(wide, low, z, high)
    fill_wide(dwide, dlow, dc, dhigh)
    fill_masks(valid, masks)
    small_ref[...] = jnp.zeros_like(small_ref)
    for r, c, size in tiles(z.shape[0]):
        own = dwide[EDGE + r : EDGE + r + size, c : c + 128]
        total = jnp.zeros((size, 128), F32)
        for i in range(KER):
            first = r + i + EDGE - RIM
            value = valid[i, r : r + size]
            term = own * (wide[first : first + size, c : c + 128] * value)
            small_ref[i : i + 1, c : c + 128] += jnp.sum(term, axis=0, keepdims=True)
            tap = taps[KER - 1 - i : KER - i, c : c + 128]
            total = total + tap * (dwide[first : first + size, c : c + 128] * value)
        dz[r : r + size, c : c + 128] = total
    a2 = normed(x2[...], gains[2:3])
    g = contract(a2, glu[...], 1, 0)
    g0, logistic = g[:, :D], jax.nn.sigmoid(g[:, D:])
    grad = dz[...]
    dg = [(grad * logistic).astype(BF16), (grad * g0 * logistic * (1.0 - logistic)).astype(BF16)]
    dn = contract(dg[0], glu[:, :D], 1, 1) + contract(dg[1], glu[:, D:], 1, 1)
    dn, gain_grad = norm_back(dn, x2[...], gains[2:3])
    small_ref[KER : KER + 1] = gain_grad
    dx2 = dx3[...] + dn
    dx2_ref[...] = dx2
    dy1 = dx2.astype(BF16)
    turned = contract(dy1, attn_out[...], 1, 0).T
    do_ref[...] = turned.astype(BF16).reshape(do_ref.shape)
    a2_ref[...] = a2
    dy1_ref[...] = dy1
    for k in range(2):
        dg_ref[:, k * D : (k + 1) * D] = dg[k]


def enter_back_kernel(
    halves, part, dt, x1, x, dx2, qkv, wi, wo, gains, *refs
):
    if halves:
        x3, gate, below = refs[:3]
        backs, refs = refs[3 : 3 + halves], refs[3 + halves :]
        dx_ref, dgate_ref = refs[:2]
        gives, refs = refs[2 : 2 + halves], refs[2 + halves :]
    else:
        dx_ref, refs = refs[0], refs[1:]
    turned, a1, a0, dy0, h0, du0, small_ref, dx1, dn0 = refs
    step = pl.program_id(0)

    @pl.when(step == 0)
    def _():
        for h in range(HEADS):
            for w in range(3):
                turned[w * D + h * HD : w * D + (h + 1) * HD] = dt[h, w]
        a1[...] = normed(x1[...], gains[1:2])
        dn, gain_grad = norm_back(contract(turned[...], qkv[...], 0, 1), x1[...], gains[1:2])
        small_ref[...] = jnp.zeros_like(small_ref)
        small_ref[1:2] = gain_grad
        grad = dx2[...] + dn
        dx1[...] = grad
        dy0[...] = (0.5 * grad).astype(BF16)
        a0[...] = normed(x[...], gains[0:1])
        dn0[...] = jnp.zeros_like(dn0)

    u = contract(a0[...], wi[...], 1, 0)
    logistic = jax.nn.sigmoid(u)
    h0[...] = (u * logistic).astype(BF16)
    slope = logistic * (1.0 + u * (1.0 - logistic))
    du = (contract(dy0[...], wo[...], 1, 0) * slope).astype(BF16)
    du0[...] = du
    dn0[...] += contract(du, wi[...], 1, 1)

    @pl.when(step == pl.num_programs(0) - 1)
    def _():
        dn, gain_grad = norm_back(dn0[...], x[...], gains[0:1])
        small_ref[0:1] = gain_grad
        dx = dx1[...] + dn
        if halves:
            _, dx4, dgate, sent, gain_grad = turn(
                dx, x3[...], gate[...], joined(part[0], backs), below[4:5]
            )
            dx_ref[...] = dx4
            dgate_ref[...] = dgate
            small_ref[4:5] = gain_grad
            give_halves(part[0], sent, gives)
        else:
            dx_ref[...] = dx.astype(BF16)


def enter_back(part, dt, x1, x, dx2, qkv, ffn_in, ffn_out, gains, below):
    rows = x.shape[0]
    column = pl.BlockSpec((D, D), lambda j, at: (0, j))
    args = [dt, x1, x, dx2, qkv, ffn_in, ffn_out, gains]
    in_specs = [None] * 5 + [column, column, None]
    stream = jax.ShapeDtypeStruct((rows, D), F32)
    if below is None:
        lead = [jax.ShapeDtypeStruct((rows, D), BF16)]
    else:
        x3, gate, halves, above = below
        args += [x3, gate, above] + list(halves)
        in_specs += [None] * (3 + len(halves))
        lead = [stream, jax.ShapeDtypeStruct((rows, 1), F32)] + half_shapes(rows)
    low = jax.ShapeDtypeStruct((rows, D), BF16)
    wide = shaped((rows, ffn_in.shape[1]), BF16)
    piece = pl.BlockSpec((rows, D), lambda j, at: (0, j))
    out = fused(
        functools.partial(enter_back_kernel, 0 if below is None else len(below[2])),
        part,
        args,
        lead
        + [shaped((3 * D, rows), BF16), low, low, low, wide, wide, jax.ShapeDtypeStruct((8, D), F32)],
        2 * rows * D * (3 * ffn_in.shape[1] + 3 * D),
        grid=(ffn_in.shape[1] // D,),
        in_specs=in_specs,
        out_specs=[None] * (len(lead) + 4) + [piece, piece, None],
        scratch=[
            pltpu.VMEM((rows, D), F32),
            pltpu.VMEM((rows, D), F32),
        ],
    )
    turned, a1, a0, dy0, h0, du0, small = out[len(lead) :]
    dqkv = dot(a1, turned, 0, 1).astype(BF16)
    dffn_in, dffn_out = dot(a0, du0, 0, 0).astype(BF16), dot(dy0, h0, 0, 0).astype(BF16)
    return out[: len(lead)], (dqkv, dffn_in, dffn_out, small)


def forward_layer(l, x, below, weights, tables, queue, coming):
    ffn_in, qkv, glu, ffn_out, attn_out, conv_out, expert, gains, taps, router = weights
    spans, rotary, own_rotary, own_spans, masks, table, onehot = tables
    rows = own_rotary.shape[-1]
    stream, low = jax.ShapeDtypeStruct((rows, D), F32), jax.ShapeDtypeStruct((rows, D), BF16)
    one = jax.ShapeDtypeStruct((rows, 1), F32)
    x, x1, heads = enter(below and below[4], x, below and below[:4], gains, ffn_in, ffn_out, qkv, own_rotary)
    heads, coming = tie(queue.point((l, -1), heads), coming)
    coming = [dense_collect(shard) for shard in coming]
    dense = [None]
    if coming:
        queue.at((l, 8), coming, lambda arrays: dense.insert(0, dense_unpack(arrays[0], UNITS)))
    queries, keys, first = heads_apart(heads)
    query_spans = spans if queries.shape[0] > 1 else own_spans[None]
    context, full, log_total = attend(query_spans, queries, keys, first)
    o = heads_together(queue.point((l, 0), context))
    x2, z = fused(
        middle_kernel, 0, [x1, o, attn_out, glu, gains], [stream, low], 6 * rows * D * D
    )
    z_low, z_high = rims(z)
    part = feature_part(isinstance(expert, list))
    x3, c, gate, *halves = fused(
        functools.partial(conv_kernel_body, len(half_shapes(rows))),
        part,
        [x2, z, z_low, z_high, masks, taps, conv_out, gains, router, onehot],
        [stream, stream, one] + half_shapes(rows),
        2 * rows * D * (D + 2 * KER),
        scratch=[pltpu.VMEM((rows + 2 * EDGE, D), F32), pltpu.VMEM((KER, rows, 128), F32)],
    )
    x3 = queue.point((l, 1), x3)
    sent = to_experts(halves, table)
    backs = from_experts(queue.point((l, 8), expert_call(sent, expert)), table)
    saved = (x, x1, queries, keys, full, log_total, o, x2, z, z_low, z_high, c, sent)
    return saved, (x3, gate, backs, gains, part), dense[0]


def backward_layer(l, grads, weights, saved, left, below, tables, queue):
    ffn_in, qkv, glu, ffn_out, attn_out, conv_out, expert, gains, taps, router = weights
    spans, rotary, own_rotary, own_spans, masks, table, onehot = tables
    x, x1, queries, keys, full, log_total, o, x2, z, z_low, z_high, c, sent = saved
    dx4, dgate, halves = grads
    x3, part = left[0], left[4]
    rows = x.shape[0]
    stream, low = jax.ShapeDtypeStruct((rows, D), F32), jax.ShapeDtypeStruct((rows, D), BF16)
    dy = queue.point((l, 2), to_experts(halves, table))
    dsent, dexpert = expert_call(sent, expert, dy)
    total = lax.psum_scatter(dexpert, PLANE, scatter_dimension=0, tiled=False)
    expert_sums = [total]
    if l == 0:
        queue.at((l, 7), [total], lambda arrays: expert_sums.insert(0, arrays[0]))
    dsent = queue.point((l, 3), dsent)
    backs = from_experts(dsent, table)
    dx3, dc, dy2, e, small_one = fused(
        functools.partial(experts_back_kernel, len(backs)),
        part,
        [dx4, dgate, x3, c, gains, router, onehot, conv_out] + list(backs),
        [stream, low, low, low, jax.ShapeDtypeStruct((2 * EXPERTS, D), F32)],
        2 * rows * D * D,
    )
    dconv_out = dot(dy2, e, 0, 0).astype(BF16)
    dc = queue.point((l, 4), dc)
    dc_low, dc_high = rims(dc)
    wide = pltpu.VMEM((rows + 2 * EDGE, D), F32)
    dx2, dheads, a2, dg, dy1, small_two = fused(
        conv_back_kernel,
        0,
        [dc, dc_low, dc_high, z, z_low, z_high, masks, taps, x2, dx3, glu, attn_out, gains],
        [
            stream,
            jax.ShapeDtypeStruct((HEADS, HD, rows), BF16),
            low,
            jax.ShapeDtypeStruct((rows, 2 * D), BF16),
            low,
            jax.ShapeDtypeStruct((KER + 1, D), F32),
        ],
        10 * rows * D * D,
        scratch=[wide, wide, pltpu.VMEM((KER, rows, 128), F32), pltpu.VMEM((rows, D), F32)],
    )
    dglu = dot(a2, dg, 0, 0).astype(BF16)
    dattn_out = dot(dy1, o, 0, 1).astype(BF16)
    early = [dglu, dattn_out, dconv_out]
    if l == 0:
        early_sums = []

        def through(arrays):
            parts = dense_both(early, arrays, flipped())
            parts = list(parts) if flipped() else [parts]
            queue.at((l, 7), parts, early_sums.extend)

        queue.at((l, 6), dense_other(early, flipped())[0], through)
    dheads = queue.point((l, 5), heads_grad(dheads))
    many = queries.shape[0] > 1
    dt = attend_back(
        spans if many else own_spans[None],
        rotary if many else own_rotary[None],
        rotary,
        queries,
        keys,
        1 if many else 0,
        dheads,
        full,
        log_total,
    )
    dt = [queue.point((l, 6), dt[0])] + list(dt[1:])
    dt = queue.point((l, 7), heads_back(dt))
    lead, (dqkv, dffn_in, dffn_out, small_three) = enter_back(
        below and below[4], dt, x1, x, dx2, qkv, ffn_in, ffn_out, gains, below and below[:4]
    )
    small = jnp.concatenate([small_one, small_two, small_three], axis=0)
    late = [dffn_in, dqkv, dffn_out]
    if l == 0:
        dense = (late, early_sums)
    else:
        dense = [dffn_in, dqkv, dglu, dffn_out, dattn_out, dconv_out]
    grads = lead[0] if below is None else (lead[0], lead[1], lead[2:])
    return grads, dense, expert_sums[0], small


def small_total(grad):
    groups = lax.axis_size(EXPERT)
    width = D // groups
    me = lax.axis_index(EXPERT)
    if flipped():
        pieces = [
            lax.dynamic_slice_in_dim(grad, (me ^ k) * width, width, axis=1) for k in range(groups)
        ]
    else:
        pieces = [grad[:, k * width : (k + 1) * width] for k in range(groups)]
    return summed_everywhere(summed(passed(pieces, EXPERT)), (HC, HX, DP))


def adamw(master, moment, square, gradient, rate, decay):
    moment_new = BETA_ONE * moment + (1.0 - BETA_ONE) * gradient
    square_new = BETA_TWO * square + (1.0 - BETA_TWO) * gradient * gradient
    unbiased = moment_new / (1.0 - BETA_ONE**STEP)
    scaled = square_new / (1.0 - BETA_TWO**STEP)
    updated = master - rate * (unbiased / (jnp.sqrt(scaled) + ADAM_EPS) + decay * master)
    return (updated, moment_new, square_new)


def expert_adamw_kernel(rates, pair, me, own_ref, other_ref, *refs):
    ins, outs = refs[:6], refs[-6:]
    grad = own_ref[...].astype(F32)
    if pair:
        grad = jnp.where(pl.program_id(0) == me[0], grad, other_ref[...].astype(F32))
    _, depth, width = grad.shape
    blocks = [grad[1, :, i : i + depth] for i in range(0, width, depth)]
    for k, value in enumerate((grad[0], jnp.concatenate(blocks, axis=0))):
        new = adamw(*[ins[3 * k + i][0, 0] for i in range(3)], value, rates[k], DECAY)
        for i in range(3):
            outs[3 * k + i][0, 0] = new[i]


def expert_adamw(l, both, states, rates, filled):
    pair = lax.axis_size(HC) == 2
    depth, width = both.shape[1], both.shape[2] // (2 if pair else 1)
    own = both[..., :width]
    other = swap(both[..., width:]) if pair else own
    me = jnp.reshape(lax.axis_index(HC), (1,)).astype(jnp.int32)
    grad = pl.BlockSpec((2, depth, width), lambda e, at: (0, 0, 0))
    specs = [pl.BlockSpec((1, 1) + s.shape[2:], lambda e, at: (l, e, 0, 0)) for s in states]
    kept = [] if filled is None else list(filled)
    return pl.pallas_call(
        functools.partial(expert_adamw_kernel, rates, pair),
        grid_spec=pltpu.PrefetchScalarGridSpec(
            num_scalar_prefetch=1,
            grid=(states[0].shape[1],),
            in_specs=[grad, grad] + specs + [pl.BlockSpec(memory_space=pl.ANY)] * len(kept),
            out_specs=specs,
        ),
        out_shape=[shaped(s.shape, F32) for s in states],
        input_output_aliases={3 + len(states) + i: i for i in range(len(kept))},
        compiler_params=pltpu.CompilerParams(vmem_limit_bytes=32 << 20),
        cost_estimate=pl.CostEstimate(
            flops=0, bytes_accessed=12 * sum(s.size for s in states) // LAYERS, transcendentals=0
        ),
    )(me, own, other, *[still(v) for v in states], *kept)


def on_device(
    frames,
    cotangent,
    lengths,
    routes,
    entry_weights,
    entry_moment,
    entry_square,
    exit_weights,
    exit_moment,
    exit_square,
    upward_weights,
    upward_moment,
    upward_square,
    downward_weights,
    downward_moment,
    downward_square,
    norm_gains,
    gains_moment,
    gains_square,
    conv_kernel,
    kernel_moment,
    kernel_square,
    router_weights,
    router_moment,
    router_square,
):
    small = jnp.concatenate(
        [norm_gains, conv_kernel, jnp.swapaxes(router_weights, 1, 2)], axis=1
    )
    if flipped():
        pieces = jnp.stack(passed([small] * 4, EXPERT))
        me = lax.axis_index(EXPERT)
        small = jnp.concatenate([take(pieces, 0, e ^ me) for e in range(4)], axis=2)
    else:
        small = lax.all_gather(small, EXPERT, axis=2, tiled=True)
    counts = (norm_gains.shape[1], conv_kernel.shape[1])
    x = to_frames(frames).astype(F32)
    upstream = to_frames(cotangent)
    tables = build_tables(lengths, routes, x.shape[0])
    shards, experts, queue = [], [], Queue()
    for l in range(LAYERS):
        shard = dense_shard(entry_weights[l], exit_weights[l])
        shards.append(shard)
        own = expert_shard(upward_weights[l], downward_weights[l])
        if l == 0 and flipped():
            experts.append([])
            across(queue, own, experts[0])
        else:
            experts.append(lax.all_gather(own, PLANE, axis=0, tiled=False))
    above = []
    queue.at((0, -1), [upstream], above.extend)
    saved, layer_weights, left = [], [], []
    for l in range(LAYERS):
        if l == 0 and flipped():
            shard = shards[0]
            first = jnp.concatenate([shard[0:4], shard[9:13]], axis=0)
            others = jnp.concatenate([shard[4:9], shard[13:15]], axis=0)
            (ffn_in, ffn_out), (x, small) = dense_gather_steps(first, (4, 4), [x, small])
            qkv, glu, attn_out, conv_out = dense_gather(others, (3, 2, 1, 1))
            dense = [ffn_in, qkv, glu, ffn_out, attn_out, conv_out]
        elif l == 0:
            dense = dense_gather(shards[0], UNITS)
        weights = tuple(dense) + (
            experts[l],
            small[l, : counts[0]],
            small[l, counts[0] : sum(counts)],
            small[l, sum(counts) :].astype(BF16),
        )
        layer_weights.append(weights)
        coming = shards[l + 1 : l + 2]
        kept, rest, dense = forward_layer(l, x, left[-1] if left else None, weights, tables, queue, coming)
        saved.append(kept)
        left.append(rest)

    rows = x.shape[0]
    x3, gate, halves, gains, part = left[-1]
    stream = jax.ShapeDtypeStruct((rows, D), F32)
    encoded, dx4, dgate, last_gain, *sent = fused(
        functools.partial(turn_kernel, len(halves)),
        part,
        [above[0], x3, gate, gains] + list(halves),
        [
            jax.ShapeDtypeStruct((rows, D), BF16),
            stream,
            jax.ShapeDtypeStruct((rows, 1), F32),
            jax.ShapeDtypeStruct((8, D), F32),
        ]
        + half_shapes(rows),
        0,
    )
    grads = (dx4, dgate, sent)
    wide_rate = 2.0 * D ** (-0.5)
    rates = (wide_rate, 2.0 * max(EFF // 64, 1) ** (-0.5))
    kernel_rate = 2.0 * KER ** (-0.5)
    states = (
        upward_weights, upward_moment, upward_square, downward_weights, downward_moment, downward_square
    )
    small_grads, dense_sums, expert_next = [last_gain], [None] * LAYERS, None
    for l in reversed(range(LAYERS)):
        below = left[l - 1] if l > 0 else None
        grads, dense, dexpert, small_grad = backward_layer(
            l, grads, layer_weights[l], saved[l], left[l], below, tables, queue
        )
        small_grads.insert(0, small_grad)
        if l > 0:
            expert_next = expert_adamw(l, dexpert, states, rates, expert_next)
            scatter_later(queue, l, dense, dense_sums)

            def update(arrays):
                nonlocal expert_next
                expert_next = arrays

            queue.at((l - 1, 7), expert_next, update)

    late, early = dense
    late, early = tie(late, passed(early if flipped() else early[0], PLANE))
    count = len(small_grads)
    after = [grads, encoded] + small_grads + dense_sums[1:]
    other, (grads, encoded, *after) = dense_other(late, flipped(), after)
    small_grad, dense_sums[1:] = jnp.concatenate(after[:count], axis=0), after[count:]
    dense_sums[1:] = [
        lax.psum_scatter(part, EXPERT, scatter_dimension=0, tiled=False) for part in dense_sums[1:]
    ]
    if flipped():
        small_grad = summed_everywhere(small_grad, (HC, HX, DP))
    else:
        small_grad = small_total(small_grad)
    late = passed(dense_both(late, other, flipped()), PLANE)
    both = from_frames(jnp.concatenate([encoded, grads], axis=0)).astype(F32)
    expert_next = expert_adamw(0, dexpert, states, rates, expert_next)
    late, others = tie(late, list(expert_next) + [both, small_grad] + dense_sums[1:])
    expert_next, (both, small_grad), dense_sums[1:] = others[:6], others[6:8], others[8:]
    encoded, input_gradient = both[:, : frames.shape[1]], both[:, frames.shape[1] :]
    parts = jnp.concatenate([summed(late), summed(early)], axis=1).astype(BF16)
    parts = [parts[k] for k in range(parts.shape[0])]
    if flipped():
        parts = [
            jnp.concatenate([own, low], axis=0) for own, low in zip(parts, small_pieces(small_grad, parts[0]))
        ]
    late, early, low = jnp.split(summed(passed(parts, EXPERT)), [11, 15], axis=0)
    if flipped():
        small_grad = low.reshape(-1, low.shape[-1])
    gains_grad, kernel_grad, router_grad = small_sums(small_grad)
    cut = [late[:7], early[:2], late[7:], early[2:]]
    dense_grad = jnp.stack([jnp.concatenate(cut, axis=0)] + [v.astype(F32) for v in dense_sums[1:]])
    entry_grad = jnp.swapaxes(dense_grad[:, 0:9], 1, 2)
    exit_grad = jnp.swapaxes(dense_grad[:, 9:], 2, 3)
    return (
        (encoded, input_gradient)
        + adamw(entry_weights, entry_moment, entry_square, entry_grad, wide_rate, DECAY)
        + adamw(exit_weights, exit_moment, exit_square, exit_grad, wide_rate, DECAY)
        + tuple(expert_next)
        + adamw(norm_gains, gains_moment, gains_square, gains_grad, 0.5, 0.0)
        + adamw(conv_kernel, kernel_moment, kernel_square, kernel_grad, kernel_rate, DECAY)
        + adamw(router_weights, router_moment, router_square, router_grad, wide_rate, DECAY)
    )


def across(queue, own, pieces):
    def halves(arrays):
        first, second = flip(arrays[1][0], PLANE, 2), flip(arrays[2][1], PLANE, 1)
        queue.at((0, 0), [first, second], lambda got: pieces.extend(list(arrays) + [jnp.stack(got)]))

    queue.at((0, -1), [own, flip(own, PLANE, 1), flip(own, PLANE, 2)], halves)


def scatter_later(queue, l, grads, sums):
    def sum_plane(arrays):
        queue.at((l - 1, 4), [dense_both(grads, arrays, False)], sum_parts)

    def sum_parts(arrays):
        sums[l] = lax.psum_scatter(arrays[0], PLANE, scatter_dimension=0, tiled=False)

    def give(arrays):
        queue.at((l - 1, 3), [swap(piece) for piece in arrays], sum_plane)

    if lax.axis_size(HC) == 1:
        sum_plane([])
    else:
        queue.at((l - 1, 2), dense_pack(grads, 1 - lax.axis_index(HC), False, True), give)


def small_pieces(grad, like):
    _, rows, width = like.shape
    grad = jnp.pad(grad.astype(BF16), ((0, -grad.shape[0] % rows), (0, 0)))
    me = lax.axis_index(EXPERT)
    cut = lambda k: lax.dynamic_slice_in_dim(grad, (me ^ k) * width, width, axis=1)
    return [cut(k).reshape(-1, rows, width) for k in range(4)]


def small_sums(total):
    each = 2 * EXPERTS + KER + 1 + 8
    gains, taps, routers = [], [], []
    for l in range(LAYERS):
        own = total[l * each : (l + 1) * each]
        over = (l + 1) * each + (each - 8 + 4 if l + 1 < LAYERS else 0)
        two, three = 2 * EXPERTS, 2 * EXPERTS + KER + 1
        gains.append(
            jnp.concatenate(
                [own[three : three + 2], own[three - 1 : three], own[EXPERTS : EXPERTS + 1], total[over : over + 1]]
            )
        )
        taps.append(own[two : two + KER])
        routers.append(own[:EXPERTS].T)
    return jnp.stack(gains), jnp.stack(taps), jnp.stack(routers)


def finer(mesh, bins):
    n_dp, n_expert, n_hidden = mesh.devices.shape
    each = bins // n_dp
    pair = EXPERTS // n_expert
    shape = (n_dp, each, n_expert // each, n_hidden // pair, pair)
    return Mesh(mesh.devices.reshape(shape), ALL)


def solution(mesh):
    hidden = (HX, HC)
    stream = P(DP, hidden, EXPERT)
    entry = P(None, (DP, HX, HC), None, EXPERT)
    leave = P(None, None, EXPERT, (DP, HX, HC))
    upward = P(None, EXPERT, DP, hidden)
    downward = P(None, EXPERT, hidden, DP)
    last = P(None, None, EXPERT)
    middle = P(None, EXPERT, None)
    states = sum([(s,) * 3 for s in (entry, leave, upward, downward, last, last, middle)], ())

    def program(*args):
        return jax.shard_map(
            on_device,
            mesh=finer(mesh, args[0].shape[0]),
            in_specs=(stream, stream, P(DP, None), P(DP, hidden, None)) + states,
            out_specs=(stream, stream) + states,
            check_vma=False,
        )(*args)

    return program
```
